32 devices in a mesh: dp: 4 (over z), context: 4 (over x, core), tensor: 2 (over y).
Axes of the slice: x: 2, y: 2, z: 4, core: 2. Of those that a mesh axis runs over, the one named last changes fastest.
Arguments:
- hidden: bfloat16 [4, 1024, 1024], P('dp', 'context'), may hold values from -6 to 6
- cotangent: bfloat16 [4, 1024, 1024], P('dp', 'context'), may hold values from -6 to 6
- norm_gain: float32 [2, 1024], replicated, may hold values from 0.25 to 1.75
- inner_proj: bfloat16 [2, 1024, 2, 2048], P(None, 'dp', None, 'tensor'), may hold values from -0.1875 to 0.1875
- state_proj: bfloat16 [2, 1024, 256], P(None, 'dp'), may hold values from -0.1875 to 0.1875
- step_proj: bfloat16 [2, 1024, 32], P(None, 'dp', 'tensor'), may hold values from -0.1875 to 0.1875
- inner_conv: float32 [2, 4, 2048], P(None, None, 'tensor'), may hold values from -3 to 3
- inner_bias: float32 [2, 2048], P(None, 'tensor'), may hold values from -1.5 to 1.5
- state_conv: float32 [2, 4, 256], replicated, may hold values from -3 to 3
- state_bias: float32 [2, 256], replicated, may hold values from -1.5 to 1.5
- step_bias: float32 [2, 32], P(None, 'tensor'), may hold values from -7 to -3
- decay_log: float32 [2, 32], P(None, 'tensor'), may hold values from 0 to 1.5
- skip_gain: float32 [2, 32], P(None, 'tensor'), may hold values from 0.5 to 1.5
- gate_gain: float32 [2, 2048], P(None, 'tensor'), may hold values from 0.25 to 1.75
- out_proj: bfloat16 [2, 2048, 1024], P(None, 'tensor', 'dp'), may hold values from -0.125 to 0.125
Outputs:
- output: bfloat16 [4, 1024, 1024], P('dp', 'context')
- hidden_grad: bfloat16 [4, 1024, 1024], P('dp', 'context')
- prenorm_grad: float32 [2, 1024], replicated
- inner_grad: float32 [2, 1024, 2, 2048], P(None, 'dp', None, 'tensor')
- state_grad: float32 [2, 1024, 256], P(None, 'dp')
- step_grad: float32 [2, 1024, 32], P(None, 'dp', 'tensor')
- kernel_grad: float32 [2, 4, 2048], P(None, None, 'tensor')
- biases_grad: float32 [2, 2048], P(None, 'tensor')
- filters_grad: float32 [2, 4, 256], replicated
- offsets_grad: float32 [2, 256], replicated
- timebias_grad: float32 [2, 32], P(None, 'tensor')
- decay_grad: float32 [2, 32], P(None, 'tensor')
- skip_grad: float32 [2, 32], P(None, 'tensor')
- gate_grad: float32 [2, 2048], P(None, 'tensor')
- outer_grad: float32 [2, 2048, 1024], P(None, 'tensor', 'dp')
The draws below stay inside these ranges and needn't reach their ends.
All inputs are finite; a program needn't handle non-finite values.
Results may differ from the reference program's by a relative error of at most 0.012.
The reference program's roundings to bfloat16 on the way count: a program that leaves them out, or rounds other values in their place, can miss the bound.
Values may be sent and summed in bfloat16 or wider, within the bound.
No kernel may reach another device: no remote copies, remote signals or barrier semaphores. Data moves between devices by JAX's collectives and lax.ppermute only.
A program may use at most 192 MiB of HBM per device.

```python
import jax
import jax.numpy as jnp
from jax import lax

D = 1024
HEADS = 32
STATE = 128
CONV = 4
BLOCK = 256
LAYERS = 2
INNER = 2048
SEQS = 4
LENGTH = 1024


def block_scale(key, extent, cuts, low, largest):
    level, own = 1.0, jax.random.fold_in(key, 6)
    for dim, blocks in cuts:
        heights = jnp.exp(jax.random.uniform(jax.random.fold_in(own, dim), (blocks,), jnp.float32, low / len(cuts), largest / len(cuts)))
        level = level * jnp.repeat(heights, extent[dim] // blocks).reshape([-1 if axis == dim else 1 for axis in range(len(extent))])
    return level


def noise(stream_key, dims, deviation, bound, shards=(), held_as=jnp.bfloat16):
    factor_of = block_scale(stream_key, dims, shards, -0.22, 0.18) if shards else 1.0
    result = jax.random.normal(stream_key, dims, jnp.float32) * deviation * factor_of
    return jnp.minimum(jnp.maximum(result, -bound), bound).astype(held_as)


def setup_inputs(seed: int = 0) -> dict:
    splits = jax.random.split(jax.random.key(seed), 16)
    return {
        "hidden": noise(splits[0], (SEQS, LENGTH, D), 1.0, 6.0, ((0, 4), (1, 4))),
        "cotangent": noise(splits[1], (SEQS, LENGTH, D), 1.0, 6.0, ((0, 4), (1, 4))),
        "norm_gain": jnp.clip(1.0 + 0.15 * jax.random.normal(splits[2], (LAYERS, D), jnp.float32), 0.25, 1.75),
        "inner_proj": noise(splits[3], (LAYERS, D, 2, INNER), D ** -0.5, 0.1875, ((1, 4), (3, 2))),
        "state_proj": noise(splits[4], (LAYERS, D, 2 * STATE), D ** -0.5, 0.1875, ((1, 4),)),
        "step_proj": noise(splits[5], (LAYERS, D, HEADS), D ** -0.5, 0.1875, ((1, 4), (2, 2))),
        "inner_conv": noise(splits[6], (LAYERS, CONV, INNER), CONV ** -0.5, 3.0, ((2, 2),), jnp.float32),
        "inner_bias": noise(splits[7], (LAYERS, INNER), 0.3, 1.5, ((1, 2),), jnp.float32),
        "state_conv": noise(splits[8], (LAYERS, CONV, 2 * STATE), CONV ** -0.5, 3.0, (), jnp.float32),
        "state_bias": noise(splits[9], (LAYERS, 2 * STATE), 0.3, 1.5, (), jnp.float32),
        "step_bias": jnp.clip(-7.0 + 4.0 * jax.random.uniform(splits[10], (LAYERS, HEADS), jnp.float32) ** block_scale(splits[10], (LAYERS, HEADS), ((1, 2),), -0.2, 0.2), -7.0, -3.0),
        "decay_log": jnp.clip(1.5 * jax.random.uniform(splits[11], (LAYERS, HEADS), jnp.float32) ** block_scale(splits[11], (LAYERS, HEADS), ((1, 2),), -0.2, 0.2), 0.0, 1.5),
        "skip_gain": jnp.clip(0.5 + 1.0 * jax.random.uniform(splits[12], (LAYERS, HEADS), jnp.float32) ** block_scale(splits[12], (LAYERS, HEADS), ((1, 2),), -0.2, 0.2), 0.5, 1.5),
        "gate_gain": jnp.clip(1.0 + 0.15 * jax.random.normal(splits[13], (LAYERS, INNER), jnp.float32), 0.25, 1.75),
        "out_proj": noise(splits[14], (LAYERS, INNER, D), INNER ** -0.5, 0.125, ((1, 2), (2, 4))),
    }


@jax.custom_vjp
def low(v):
    return lax.optimization_barrier(v.astype(jnp.bfloat16)).astype(jnp.float32)

@jax.custom_vjp
def low_back(v):
    return v

def low_keep(v):
    return (low(v), None)

def low_pass(kept, grad):
    return (grad,)

def back_keep(v):
    return (v, None)

def back_low(kept, grad):
    return (low(grad),)
low.defvjp(low_keep, low_pass)
low_back.defvjp(back_keep, back_low)
eps_norm = 1e-05
highest = lax.Precision.HIGHEST

def causal_conv(values, kernel, offset):
    support = kernel.shape[0]
    length_here = values.shape[0]
    padded = jnp.pad(values, ((support - 1, 0), (0, 0)))
    running = offset
    for shift_index in range(support):
        running = running + kernel[shift_index] * padded[shift_index:shift_index + length_here]
    return running

def block_step(carried, pieces):
    inner_heads, step_size, log_rates, input_mat, output_mat = pieces
    count_here = inner_heads.shape[0]
    cumulative = jnp.cumsum(log_rates, axis=0).T
    row_index = lax.broadcasted_iota(jnp.int32, (count_here, count_here), 0)
    col_index = lax.broadcasted_iota(jnp.int32, (count_here, count_here), 1)
    causal = row_index >= col_index
    log_gaps = cumulative[:, :, None] - cumulative[:, None, :]
    decays = jnp.where(causal, jnp.exp(jnp.where(causal, log_gaps, 0.0)), 0.0)
    scores = jnp.dot(output_mat, input_mat.T, precision=highest)
    weighted = inner_heads * step_size[:, :, None]
    intra_part = jnp.einsum('htu,uhp->thp', scores[None] * decays, weighted, precision=highest)
    inter_part = jnp.exp(cumulative.T)[:, :, None] * jnp.einsum('tn,hpn->thp', output_mat, carried, precision=highest)
    tail_decay = jnp.exp(cumulative[:, -1:] - cumulative)
    local_state = jnp.einsum('hu,uhp,un->hpn', tail_decay, weighted, input_mat, precision=highest)
    following = jnp.exp(cumulative[:, -1])[:, None, None] * carried + local_state
    return (following, intra_part + inter_part)

def layer(hidden_in, params):
    norm_scale, inner_proj, state_proj, step_proj, inner_conv, inner_bias, state_conv, state_bias, step_bias, decay_log, skip_gain, gate_gain, out_proj = params
    length_here = hidden_in.shape[0]
    heads_total = decay_log.shape[0]
    state_size = state_proj.shape[1] // 2
    norm_one = lax.rsqrt(lax.optimization_barrier(jnp.mean(hidden_in * hidden_in, axis=-1, keepdims=True)) + eps_norm)
    normed = low(hidden_in * norm_one * norm_scale)
    gate_pre = low_back(jnp.dot(normed, inner_proj[:, 0], precision=highest))
    inner_pre = low_back(jnp.dot(normed, inner_proj[:, 1], precision=highest))
    state_pre = low_back(jnp.dot(normed, state_proj, precision=highest))
    step_pre = low_back(jnp.dot(normed, step_proj, precision=highest))
    inner_act = jax.nn.silu(causal_conv(inner_pre, inner_conv, inner_bias))
    state_act = jax.nn.silu(causal_conv(state_pre, state_conv, state_bias))
    step_size = jax.nn.softplus(step_pre + step_bias)
    log_rates = -step_size * jnp.exp(decay_log)
    inner_heads = inner_act.reshape(length_here, heads_total, -1)
    head_width = inner_heads.shape[2]
    blocks = length_here // BLOCK
    pieces = (inner_heads.reshape(blocks, BLOCK, heads_total, head_width), step_size.reshape(blocks, BLOCK, heads_total), log_rates.reshape(blocks, BLOCK, heads_total), state_act[:, :state_size].reshape(blocks, BLOCK, state_size), state_act[:, state_size:].reshape(blocks, BLOCK, state_size))
    start_state = jnp.zeros((heads_total, head_width, state_size), jnp.float32)
    unused, scanned = lax.scan(jax.checkpoint(block_step), start_state, pieces)
    scan_out = scanned.reshape(length_here, heads_total, head_width) + skip_gain[:, None] * inner_heads
    product = scan_out.reshape(length_here, -1) * jax.nn.silu(gate_pre)
    norm_two = lax.rsqrt(lax.optimization_barrier(jnp.mean(product * product, axis=-1, keepdims=True)) + eps_norm)
    normed_out = low(product * norm_two * gate_gain)
    return hidden_in + low_back(jnp.dot(normed_out, out_proj, precision=highest))

def reference(hidden, cotangent, norm_gain, inner_proj, state_proj, step_proj, inner_conv, inner_bias, state_conv, state_bias, step_bias, decay_log, skip_gain, gate_gain, out_proj):
    params = tuple((member.astype(jnp.float32) for member in (norm_gain, inner_proj, state_proj, step_proj, inner_conv, inner_bias, state_conv, state_bias, step_bias, decay_log, skip_gain, gate_gain, out_proj)))

    def network(sequence, weights):
        for layer_index in range(LAYERS):
            sequence = layer(sequence, tuple((member[layer_index] for member in weights)))
        return sequence

    def per_sequence(totals, pieces):
        sequence, cotangent_row = pieces
        result_seq, pullback = jax.vjp(network, sequence.astype(jnp.float32), params)
        seq_grad, param_grads = pullback(cotangent_row.astype(jnp.float32))
        totals = jax.tree.map(jnp.add, totals, param_grads)
        return (totals, (result_seq.astype(jnp.bfloat16), seq_grad.astype(jnp.bfloat16)))
    zero_grads = jax.tree.map(jnp.zeros_like, params)
    totals, outputs = lax.scan(per_sequence, zero_grads, (hidden, cotangent))
    return (outputs[0], outputs[1], totals[0], totals[1], totals[2], totals[3], totals[4], totals[5], totals[6], totals[7], totals[8], totals[9], totals[10], totals[11], totals[12])
```

```python
import jax
import jax.numpy as jnp
from jax import lax
from jax.sharding import PartitionSpec as P

eps_norm = 1e-05
low = jnp.bfloat16
wide = jnp.float32


def swapped(value, axis, bit):
    return lax.ppermute(value, axis, [(i, i ^ bit) for i in range(lax.axis_size(axis))])


def shifted(value, axis, distance):
    count = lax.axis_size(axis)
    return lax.ppermute(
        value, axis, [(i, i + distance) for i in range(count) if 0 <= i + distance < count]
    )


def bits_of(axis):
    count = lax.axis_size(axis)
    assert count & (count - 1) == 0
    return [1 << k for k in range(count.bit_length() - 1)]


def spread(piece):
    pieces = {0: piece}
    for bit in reversed(bits_of("context")):
        for r in list(pieces):
            pieces[r | bit] = swapped(pieces[r], "context", bit)
    return [pieces[r] for r in range(len(pieces))]


def reduced(parts):
    parts = dict(enumerate(parts))
    for bit in bits_of("context"):
        for r in sorted(parts):
            if r & bit:
                parts[r ^ bit] = parts[r ^ bit] + swapped(
                    parts[r].astype(low), "context", bit
                ).astype(wide)
        parts = {r: part for r, part in parts.items() if not r & bit}
    return lax.psum_scatter(parts[0].astype(low), "dp", scatter_dimension=0, tiled=True)


def in_order(pieces):
    me = lax.axis_index("context")
    stacked = jnp.stack(pieces)
    return jnp.concatenate(
        [lax.dynamic_index_in_dim(stacked, q ^ me, keepdims=False) for q in range(len(pieces))]
    )


def to_local(value):
    me, count, shards = lax.axis_index("context"), lax.axis_size("context"), lax.axis_size("dp")
    lead = value.shape[:-1]
    cut = value.reshape(lead + (shards, count, -1))
    axis = len(lead) + 1
    return jnp.concatenate(
        [
            lax.dynamic_index_in_dim(cut, r ^ me, axis, keepdims=False).reshape(lead + (-1,))
            for r in range(count)
        ],
        axis=-1,
    )


def from_local(value):
    me, count, shards = lax.axis_index("context"), lax.axis_size("context"), lax.axis_size("dp")
    lead = value.shape[:-1]
    cut = value.reshape(lead + (count, shards, -1))
    axis = len(lead)
    return jnp.stack(
        [lax.dynamic_index_in_dim(cut, q ^ me, axis, keepdims=False) for q in range(count)],
        axis=axis + 1,
    ).reshape(value.shape)


def chunks(value):
    return jnp.split(value, lax.axis_size("context"), axis=-1)


def product_in(rows, pieces):
    total = 0.0
    for part, piece in zip(chunks(rows), pieces):
        total = total + jnp.dot(part, piece, preferred_element_type=wide)
    return total


def product_out(values, pieces):
    return jnp.concatenate(
        [
            lax.dot_general(values, piece, (((1,), (1,)), ((), ())), preferred_element_type=wide)
            for piece in pieces
        ],
        axis=-1,
    )


def product_grad(rows, values):
    return [
        lax.dot_general(part, values, (((0,), (0,)), ((), ())), preferred_element_type=wide)
        for part in chunks(rows)
    ]


def tensor_sum(value):
    mine = value.astype(low)
    total = mine.astype(wide)
    other = mine
    for bit in bits_of("tensor"):
        other = swapped(total.astype(low), "tensor", bit)
        total = total.astype(low).astype(wide) + other.astype(wide)
    return total


def chained(decay, value, direction):
    carried = jnp.zeros_like(value)
    count = lax.axis_size("context")
    for step in range(count - 1):
        source = step if direction == 1 else count - 1 - step
        sent = (decay * carried + value).astype(low)
        carried = carried + lax.ppermute(
            sent, "context", [(source, source + direction)]
        ).astype(wide)
    return carried


def silu_grad(inputs):
    sigmoid_value = jax.nn.sigmoid(inputs)
    return sigmoid_value * (1.0 + inputs * (1.0 - sigmoid_value))


def causal_conv(padded, kernel, offset):
    length_here = padded.shape[0] - kernel.shape[0] + 1
    running = offset
    for k in range(kernel.shape[0]):
        running = running + kernel[k] * padded[k : k + length_here]
    return running


def conv_back(padded, kernel, gradient):
    support, length_here = kernel.shape[0], gradient.shape[0]
    spread_rows = jnp.zeros(padded.shape, wide)
    kernel_parts = []
    for k in range(support):
        spread_rows = spread_rows + jnp.pad(kernel[k] * gradient, ((k, support - 1 - k), (0, 0)))
        kernel_parts.append(jnp.sum(padded[k : k + length_here] * gradient, axis=0))
    return (spread_rows, jnp.stack(kernel_parts), jnp.sum(gradient, axis=0))


def decay_table(cumulative):
    length_here = cumulative.shape[-1]
    row_index = lax.broadcasted_iota(jnp.int32, (length_here, length_here), 0)
    col_index = lax.broadcasted_iota(jnp.int32, (length_here, length_here), 1)
    causal = row_index >= col_index
    log_gaps = cumulative[..., :, None] - cumulative[..., None, :]
    return jnp.where(causal, jnp.exp(jnp.where(causal, log_gaps, 0.0)), 0.0)


def layer_forward(hidden_in, weights, params):
    scan_weights, gate_weights, out_weights = weights
    (norm_scale, taps, tap_bias, step_bias, decay_log, skip_gain, gate_gain) = params
    length_here = hidden_in.shape[0]
    support, inner = taps.shape[0], gate_gain.shape[0]
    heads_here = decay_log.shape[0]
    mixed = taps.shape[1]
    state_size = (mixed - inner) // 2
    norm_one = lax.rsqrt(jnp.mean(hidden_in * hidden_in, axis=-1, keepdims=True) + eps_norm)
    normed = (hidden_in * norm_one * norm_scale).astype(low)
    scan_pre = product_in(normed, scan_weights)
    conv_pre, step_pre = scan_pre[:, :mixed], scan_pre[:, mixed:].T
    edge_rows = shifted(conv_pre[length_here - support + 1 :], "context", 1)
    gate_pre = product_in(normed, gate_weights)
    padded = jnp.concatenate([edge_rows, conv_pre], axis=0)
    lin = causal_conv(padded, taps, tap_bias)
    acted = jax.nn.silu(lin)
    heads_t = acted[:, :inner].T.reshape(heads_here, -1, length_here)
    input_m = acted[:, inner : inner + state_size]
    output_m = acted[:, inner + state_size :]
    step_size = jax.nn.softplus(step_pre + step_bias[:, None])
    decay_rate = jnp.exp(decay_log)
    cumulative = jnp.cumsum(-step_size * decay_rate[:, None], axis=-1)
    tail_decay = jnp.exp(cumulative[..., -1:] - cumulative)
    weighted = heads_t * step_size[:, None, :]
    local_state = jnp.einsum("hpu,un->hpn", weighted * tail_decay[:, None, :], input_m)
    block_decay = jnp.exp(cumulative[:, -1])[:, None, None]
    carried = chained(block_decay, local_state, 1)
    decays = decay_table(cumulative)
    scores = jnp.dot(output_m, input_m.T)
    intra_part = jnp.einsum("htu,hpu->hpt", scores[None] * decays, weighted)
    rise_decay = jnp.exp(cumulative)
    inter_part = rise_decay[:, None, :] * jnp.einsum("hpn,tn->hpt", carried, output_m)
    scan_heads = intra_part + inter_part + skip_gain[:, None, None] * heads_t
    scan_out = scan_heads.reshape(-1, length_here).T
    gate_act = jax.nn.silu(gate_pre)
    product = scan_out * gate_act
    inner_total = inner * lax.axis_size("tensor")
    squares = jnp.sum(product * product, axis=-1)
    for bit in bits_of("tensor"):
        squares = squares + swapped(squares, "tensor", bit)
    norm_two = lax.rsqrt(squares / inner_total + eps_norm)[:, None]
    branch = tensor_sum(product_out((product * gate_gain).astype(low), out_weights))
    stored = (
        hidden_in, norm_one, normed, gate_pre, padded, lin, step_pre, step_size, heads_t, weighted,
        input_m, output_m, cumulative, scores, tail_decay, block_decay, carried, rise_decay,
        inter_part, scan_out, gate_act, product, norm_two, branch,
    )
    return (hidden_in + norm_two * branch, stored)


def layer_backward(gradient, weights, params, stored):
    scan_weights, gate_weights, out_weights = weights
    (norm_scale, taps, tap_bias, step_bias, decay_log, skip_gain, gate_gain) = params
    (
        hidden_in, norm_one, normed, gate_pre, padded, lin, step_pre, step_size, heads_t, weighted,
        input_m, output_m, cumulative, scores, tail_decay, block_decay, carried, rise_decay,
        inter_part, scan_out, gate_act, product, norm_two, branch,
    ) = stored
    length_here = hidden_in.shape[0]
    support, inner = taps.shape[0], gate_gain.shape[0]
    heads_here = decay_log.shape[0]
    inner_total = inner * lax.axis_size("tensor")
    grad_low = gradient.astype(low)
    normed_out = (product * norm_two * gate_gain).astype(low)
    outer_part = reduced(product_grad(grad_low, normed_out))
    grad_normed_out = product_in(grad_low, out_weights)
    gate_grad = jnp.sum(grad_normed_out * product * norm_two, axis=0)
    scaled = grad_normed_out * gate_gain
    inner_dot = jnp.sum(grad_low.astype(wide) * branch, axis=-1, keepdims=True)
    grad_product = norm_two * scaled - product * norm_two**3 * (inner_dot / inner_total)
    grad_scan = (grad_product * gate_act).T.reshape(heads_here, -1, length_here)
    grad_gate = (grad_product * scan_out * silu_grad(gate_pre)).astype(low)
    lifted = grad_scan * rise_decay[:, None, :]
    grad_carried = jnp.einsum("hpt,tn->hpn", lifted, output_m)
    following = chained(block_decay, grad_carried, -1)
    gate_part = reduced(product_grad(normed, grad_gate))
    skip_grad = jnp.sum(grad_scan * heads_t, axis=(1, 2))
    grad_output = jnp.einsum("hpn,hpt->tn", carried, lifted)
    grad_cumul = jnp.sum(grad_scan * inter_part, axis=1)
    decays = decay_table(cumulative)
    mixing = scores[None] * decays
    grad_mixing = jnp.einsum("hpt,hpu->htu", grad_scan, weighted)
    grad_scores = jnp.sum(grad_mixing * decays, axis=0)
    through = grad_mixing * mixing
    along_input = jnp.einsum("hpn,un->hpu", following, input_m)
    grad_weighted = tail_decay[:, None, :] * along_input + jnp.einsum(
        "htu,hpt->hpu", mixing, grad_scan
    )
    grad_block = jnp.sum(following * carried, axis=(1, 2))
    grad_input = jnp.einsum("hpu,hpn->un", weighted * tail_decay[:, None, :], following)
    grad_tail = jnp.sum(weighted * along_input, axis=1) * tail_decay
    last_extra = jnp.sum(grad_tail, axis=-1) + grad_block * block_decay[:, 0, 0]
    last_mark = (lax.broadcasted_iota(jnp.int32, (length_here,), 0) == length_here - 1).astype(wide)
    grad_cumul = (
        grad_cumul - grad_tail + jnp.sum(through, axis=2) - jnp.sum(through, axis=1)
        + last_extra[..., None] * last_mark
    )
    grad_output = grad_output + jnp.dot(grad_scores, input_m)
    grad_input = grad_input + jnp.dot(grad_scores.T, output_m)
    grad_rate = jnp.flip(jnp.cumsum(jnp.flip(grad_cumul, -1), axis=-1), -1)
    decay_rate = jnp.exp(decay_log)
    grad_steps = -grad_rate * decay_rate[:, None] + jnp.sum(grad_weighted * heads_t, axis=1)
    decay_grad = -jnp.sum(grad_rate * step_size, axis=1) * decay_rate
    grad_heads = skip_gain[:, None, None] * grad_scan + grad_weighted * step_size[:, None, :]
    grad_step_pre = grad_steps * jax.nn.sigmoid(step_pre + step_bias[:, None])
    timebias_grad = jnp.sum(grad_step_pre, axis=1)
    grad_lin = jnp.concatenate(
        [grad_heads.reshape(-1, length_here).T, grad_input, grad_output], axis=1
    ) * silu_grad(lin)
    spread_rows, taps_grad, tap_bias_grad = conv_back(padded, taps, grad_lin)
    arrived = shifted(spread_rows[: support - 1], "context", -1)
    grad_conv = spread_rows[support - 1 :] + jnp.pad(
        arrived, ((length_here - support + 1, 0), (0, 0))
    )
    grad_scan_pre = jnp.concatenate([grad_conv, grad_step_pre.T], axis=1).astype(low)
    scan_part = reduced(product_grad(normed, grad_scan_pre))
    grad_normed = tensor_sum(
        product_out(grad_scan_pre, scan_weights) + product_out(grad_gate, gate_weights)
    )
    prenorm_grad = jnp.sum(grad_normed * hidden_in * norm_one, axis=0)
    scaled_in = grad_normed * norm_scale
    grad_hidden = (
        gradient
        + norm_one * scaled_in
        - hidden_in * norm_one**3 * jnp.mean(scaled_in * hidden_in, axis=-1, keepdims=True)
    )
    state_part = scan_part[:, inner : taps.shape[1]].astype(wide)
    for bit in bits_of("tensor"):
        state_part = state_part + swapped(state_part.astype(low), "tensor", bit).astype(wide)
    large_part = (outer_part, gate_part, scan_part, state_part.astype(low))
    small_part = (
        from_local(prenorm_grad),
        taps_grad[:, :inner],
        tap_bias_grad[:inner],
        taps_grad[:, inner:],
        tap_bias_grad[inner:],
        timebias_grad,
        decay_grad,
        skip_grad,
        gate_grad,
    )
    return (grad_hidden, large_part, small_part)


def on_device(
    hidden,
    cotangent,
    norm_gain,
    inner_proj,
    state_proj,
    step_proj,
    inner_conv,
    inner_bias,
    state_conv,
    state_bias,
    step_bias,
    decay_log,
    skip_gain,
    gate_gain,
    out_proj,
):
    layers_here = inner_proj.shape[0]
    me, count = lax.axis_index("context"), lax.axis_size("context")
    rows = inner_proj.shape[1] // count

    def quarter(value, axis):
        return lax.dynamic_slice_in_dim(value, me * rows, rows, axis)

    inner_q, state_q, step_q = (quarter(v, 1) for v in (inner_proj, state_proj, step_proj))
    out_q = quarter(out_proj, 2)
    layer_weights = []
    for layer in range(layers_here):
        scan_q = jnp.concatenate([inner_q[layer, :, 1], state_q[layer], step_q[layer]], axis=1)
        layer_weights.append(
            [
                spread(lax.all_gather(piece, "dp", axis=0, tiled=True))
                for piece in (scan_q, inner_q[layer, :, 0], out_q[layer].T)
            ]
        )
    taps = jnp.concatenate([inner_conv, state_conv], axis=-1)
    tap_bias = jnp.concatenate([inner_bias, state_bias], axis=-1)
    gains = to_local(norm_gain)
    current = to_local(hidden[0]).astype(wide)
    kept_stored = []
    layer_params = []
    for layer in range(layers_here):
        layer_params.append(
            tuple(
                v[layer] for v in (gains, taps, tap_bias, step_bias, decay_log, skip_gain, gate_gain)
            )
        )
        current, stored = layer_forward(current, layer_weights[layer], layer_params[layer])
        kept_stored.append(stored)
    output = from_local(current.astype(low))
    gradient = to_local(cotangent[0]).astype(wide)
    large_grads = [None] * layers_here
    small_grads = [None] * layers_here
    for layer in reversed(range(layers_here)):
        gradient, large_part, small_grads[layer] = layer_backward(
            gradient, layer_weights[layer], layer_params[layer], kept_stored[layer]
        )
        large_grads[layer] = [in_order(spread(part)).astype(wide) for part in large_part]
    stacked = [jnp.stack([member[i] for member in small_grads]) for i in range(9)]
    everywhere = ("dp", "context", "tensor")
    filters_grad, offsets_grad = lax.psum((stacked[3], stacked[4]), everywhere)
    summed = lax.psum(
        tuple(v for i, v in enumerate(stacked) if i not in (3, 4)), ("dp", "context")
    )
    inner = gate_gain.shape[1]
    mixed = taps.shape[-1]
    return (
        output[None],
        from_local(gradient.astype(low))[None],
        summed[0],
        jnp.stack([jnp.stack([m[1], m[2][:, :inner]], axis=1) for m in large_grads]),
        jnp.stack([m[3] for m in large_grads]),
        jnp.stack([m[2][:, mixed:] for m in large_grads]),
        summed[1],
        summed[2],
        filters_grad,
        offsets_grad,
        summed[3],
        summed[4],
        summed[5],
        summed[6],
        jnp.stack([m[0].T for m in large_grads]),
    )


def solution(mesh):
    return jax.shard_map(
        on_device,
        mesh=mesh,
        in_specs=(
            P("dp", "context", None),
            P("dp", "context", None),
            P(),
            P(None, "dp", None, "tensor"),
            P(None, "dp", None),
            P(None, "dp", "tensor"),
            P(None, None, "tensor"),
            P(None, "tensor"),
            P(),
            P(),
            P(None, "tensor"),
            P(None, "tensor"),
            P(None, "tensor"),
            P(None, "tensor"),
            P(None, "tensor", "dp"),
        ),
        out_specs=(
            P("dp", "context", None),
            P("dp", "context", None),
            P(),
            P(None, "dp", None, "tensor"),
            P(None, "dp", None),
            P(None, "dp", "tensor"),
            P(None, None, "tensor"),
            P(None, "tensor"),
            P(),
            P(),
            P(None, "tensor"),
            P(None, "tensor"),
            P(None, "tensor"),
            P(None, "tensor"),
            P(None, "tensor", "dp"),
        ),
        check_vma=False,
    )
```

```python
import functools

import jax
import jax.numpy as jnp
from jax import lax
from jax.experimental import pallas as pl
from jax.experimental.pallas import tpu as pltpu
from jax.sharding import PartitionSpec as P

eps_norm = 1e-05
low = jnp.bfloat16
wide = jnp.float32


def swapped(value, axis, bit):
    return lax.ppermute(value, axis, [(i, i ^ bit) for i in range(lax.axis_size(axis))])


def shifted(value, axis, distance):
    count = lax.axis_size(axis)
    return lax.ppermute(
        value, axis, [(i, i + distance) for i in range(count) if 0 <= i + distance < count]
    )


def bits_of(axis):
    count = lax.axis_size(axis)
    assert count & (count - 1) == 0
    return [1 << k for k in range(count.bit_length() - 1)]


def spread(piece):
    pieces = {0: piece}
    for bit in reversed(bits_of("context")):
        for r in list(pieces):
            pieces[r | bit] = swapped(pieces[r], "context", bit)
    return [pieces[r] for r in range(len(pieces))]


def reduced(parts):
    parts = dict(enumerate(parts))
    for bit in bits_of("context"):
        for r in sorted(parts):
            if r & bit:
                parts[r ^ bit] = parts[r ^ bit].astype(wide) + swapped(
                    parts[r].astype(low), "context", bit
                ).astype(wide)
        parts = {r: part for r, part in parts.items() if not r & bit}
    return lax.psum_scatter(parts[0].astype(low), "dp", scatter_dimension=0, tiled=True)


def gathered(piece):
    count, me = lax.axis_size("dp"), lax.axis_index("dp")
    if count > 4 or piece.size > 2**17:
        return lax.all_gather(piece, "dp", axis=0, tiled=True)
    ring = [(i, (i + 1) % count) for i in range(count)]
    held = [piece]
    for step in range(count - 1):
        held.append(lax.ppermute(held[-1], "dp", ring))
    stacked = jnp.stack(held)
    return jnp.concatenate(
        [lax.dynamic_index_in_dim(stacked, (me - j) % count, keepdims=False) for j in range(count)]
    )


def everywhere(parts, axes):
    rows = -(-sum(part.size for part in parts) // 1024)
    flat = jnp.concatenate([part.reshape(-1) for part in parts])
    packed = jnp.pad(flat, (0, rows * 1024 - flat.size)).reshape(rows * 8, 128)
    for axis in axes:
        for bit in bits_of(axis):
            packed = packed + swapped(packed, axis, bit)
    flat = packed.reshape(-1)
    result, place = [], 0
    for part in parts:
        result.append(flat[place : place + part.size].reshape(part.shape))
        place += part.size
    return result


def in_order(pieces):
    me = lax.axis_index("context")
    stacked = jnp.stack(pieces)
    return jnp.concatenate(
        [lax.dynamic_index_in_dim(stacked, q ^ me, keepdims=False) for q in range(len(pieces))]
    )


def to_local(value):
    me, count, shards = lax.axis_index("context"), lax.axis_size("context"), lax.axis_size("dp")
    lead = value.shape[:-1]
    cut = value.reshape(lead + (shards, count, -1))
    axis = len(lead) + 1
    return jnp.concatenate(
        [
            lax.dynamic_index_in_dim(cut, r ^ me, axis, keepdims=False).reshape(lead + (-1,))
            for r in range(count)
        ],
        axis=-1,
    )


def from_local(value):
    me, count, shards = lax.axis_index("context"), lax.axis_size("context"), lax.axis_size("dp")
    lead = value.shape[:-1]
    cut = value.reshape(lead + (count, shards, -1))
    axis = len(lead)
    return jnp.stack(
        [lax.dynamic_index_in_dim(cut, q ^ me, axis, keepdims=False) for q in range(count)],
        axis=axis + 1,
    ).reshape(value.shape)


def dot(left, right, contract=(1, 0)):
    return lax.dot_general(
        left.astype(low),
        right.astype(low),
        (((contract[0],), (contract[1],)), ((), ())),
        preferred_element_type=wide,
    )


def split(value, count):
    terms = []
    for _ in range(count):
        terms.append(value.astype(low))
        value = value - terms[-1].astype(wide)
    return terms


def triangle(length, later):
    row = lax.broadcasted_iota(jnp.int32, (length, length), 0)
    col = lax.broadcasted_iota(jnp.int32, (length, length), 1)
    return row <= col if later else row >= col


def running(value, later=False):
    table = jnp.where(triangle(value.shape[0], later), 1.0, 0.0)
    return sum(dot(table, term) for term in split(value, 3))


def running_t(value):
    table = jnp.where(triangle(value.shape[0], False), 1.0, 0.0)
    return sum(dot(term, table, (0, 1)) for term in split(value, 3))


def heads_table(heads, inner):
    row = lax.broadcasted_iota(jnp.int32, (heads, inner), 0)
    col = lax.broadcasted_iota(jnp.int32, (heads, inner), 1)
    width = inner // heads
    return jnp.where((col >= row * width) & (col < (row + 1) * width), 1.0, 0.0)


def to_channels(value, table):
    return sum(dot(term, table) for term in split(value, 2))


def to_heads(value, table):
    return sum(dot(term, table, (1, 1)) for term in split(value, 2))


def silu_grad(inputs):
    sigmoid_value = jax.nn.sigmoid(inputs)
    return sigmoid_value * (1.0 + inputs * (1.0 - sigmoid_value))


def silu(inputs):
    return inputs * jax.nn.sigmoid(inputs)


def softplus(inputs):
    return jnp.maximum(inputs, 0.0) + jnp.log1p(jnp.exp(-jnp.abs(inputs)))


def total_rows(value):
    return jnp.sum(value, axis=0, keepdims=True)


def total_cols(value):
    return jnp.sum(value, axis=1, keepdims=True)


def call(body, operands, results, scratch=(), flops=10**9):
    shapes = [jax.ShapeDtypeStruct(shape, kind) for shape, kind in results]
    size = sum(v.size * v.dtype.itemsize for v in list(operands) + shapes)
    return pl.pallas_call(
        body,
        out_shape=shapes,
        scratch_shapes=[pltpu.VMEM(shape, kind) for shape, kind in scratch],
        compiler_params=pltpu.CompilerParams(vmem_limit_bytes=48 * 2**20),
        cost_estimate=pl.CostEstimate(flops=flops, bytes_accessed=size, transcendentals=0),
    )(*operands)


def gate_norm(inner_total, squares, squares_other):
    return lax.rsqrt((squares + squares_other) / inner_total + eps_norm)


def enter_body(count, inner_total, mixed, combine, *refs):
    refs = list(refs)
    if combine:
        hidden_ref, mine_ref, other_ref, squares_ref, squares_other_ref = refs[:5]
        del refs[:5]
        norm_two = gate_norm(inner_total, squares_ref[...], squares_other_ref[...])
        branch = mine_ref[...].astype(wide) + other_ref[...].astype(wide)
        hidden = hidden_ref[...] + norm_two * branch
        refs[-1][...] = hidden
        del refs[-1]
    else:
        hidden = refs[0][...].astype(wide)
        del refs[0]
    gain_ref, weights, (norm_ref, normed_ref, conv_ref, step_ref) = refs[0], refs[1:-4], refs[-4:]
    norm_one = lax.rsqrt(
        total_cols(hidden * hidden) / hidden.shape[1] + eps_norm
    )
    normed = (hidden * norm_one * gain_ref[...]).astype(low)
    norm_ref[...] = norm_one
    normed_ref[...] = normed
    width = hidden.shape[1] // count
    total = 0.0
    for r in range(count):
        total = total + dot(normed[:, r * width : (r + 1) * width], weights[r][...])
    conv_ref[...] = total[:, :mixed]
    step_ref[...] = total[:, mixed:]


def states_body(
    inner, conv_ref, edge_ref, taps_ref, bias_ref, step_ref, step_bias_ref, decay_ref,
    lin_ref, dt_ref, cs_ref, cst_ref, state_ref, low_ref, block_ref, ext_ref,
):
    length, mixed = conv_ref.shape
    size = (mixed - inner) // 2
    heads = step_ref.shape[1]
    ext_ref[:8] = edge_ref[...]
    ext_ref[8:] = conv_ref[...]
    support = taps_ref.shape[0]
    lin = bias_ref[...]
    for k in range(support):
        first = 9 - support + k
        lin = lin + taps_ref[k : k + 1, :] * ext_ref[first : first + length, :]
    lin_ref[...] = lin
    dt = softplus(step_ref[...] + step_bias_ref[...])
    rate = -dt * jnp.exp(decay_ref[...])
    cs = running(rate)
    last = cs[length - 1 :, :]
    dt_ref[...] = dt
    cs_ref[...] = cs
    cst_ref[...] = running_t(rate)
    table = heads_table(heads, inner)
    tailed = silu(lin[:, :inner]) * to_channels(dt * jnp.exp(last - cs), table)
    state = dot(silu(lin[:, inner : inner + size]), tailed, (0, 0))
    state_ref[...] = state
    low_ref[...] = state.astype(low)
    block_ref[...] = to_channels(jnp.broadcast_to(jnp.exp(last), (8, heads)), table)[:1]


def intra_body(inner, count, *refs):
    lin_ref, dt_ref, cs_ref, cst_ref, skip_ref, normed_ref = refs[:6]
    weights, (y_ref, gate_ref) = refs[6:-2], refs[-2:]
    length, mixed = lin_ref.shape
    size = (mixed - inner) // 2
    heads = dt_ref.shape[1]
    width = inner // heads
    table = heads_table(heads, inner)
    inputs = silu(lin_ref[:, inner : inner + size])
    outputs = silu(lin_ref[:, inner + size :])
    scores = dot(outputs, inputs, (1, 1))
    causal = triangle(length, False)
    x = silu(lin_ref[:, :inner])
    weighted = (x * to_channels(dt_ref[...], table)).astype(low)
    skipped = x * to_channels(skip_ref[...], table)[:1]
    lane = lax.broadcasted_iota(jnp.int32, (length, 2 * width), 1)
    for pair in range(heads // 2):
        columns = slice(pair * 2 * width, (pair + 1) * 2 * width)
        parts = []
        for head in (2 * pair, 2 * pair + 1):
            gaps = cs_ref[:, head : head + 1] - cst_ref[head : head + 1, :]
            mixing = scores * jnp.exp(jnp.where(causal, gaps, -1e30))
            parts.append(dot(mixing, weighted[:, columns]))
        y_ref[:, columns] = jnp.where(lane < width, *parts) + skipped[:, columns]
    total = 0.0
    step = normed_ref.shape[1] // count
    for r in range(count):
        total = total + dot(normed_ref[:, r * step : (r + 1) * step], weights[r][...])
    gate_ref[...] = total


def leave_body(inner, count, *refs):
    lin_ref, cs_ref, y_ref, carried_ref, gate_ref, gain_ref = refs[:6]
    weights, (y_out_ref, squares_ref, out_ref) = refs[6:-3], refs[-3:]
    size = carried_ref.shape[0]
    heads = cs_ref.shape[1]
    table = heads_table(heads, inner)
    outputs = silu(lin_ref[:, inner + size :])
    rise = to_channels(jnp.exp(cs_ref[...]), table)
    y = y_ref[...] + rise * dot(outputs, carried_ref[...])
    y_out_ref[...] = y
    product = y * silu(gate_ref[...])
    squares_ref[...] = total_cols(product * product)
    gained = (product * gain_ref[...]).astype(low)
    step = out_ref.shape[1] // count
    for r in range(count):
        out_ref[:, r * step : (r + 1) * step] = dot(gained, weights[r][...], (1, 1)).astype(low)


def gate_back_body(inner, inner_total, count, *refs):
    (grad_ref, lin_ref, cs_ref, y_ref, gate_ref, gain_ref, squares_ref, squares_other_ref,
     mine_ref, other_ref) = refs[:10]
    weights = refs[10 : 10 + count]
    (grad_low_ref, normed_out_ref, gate_grad_ref, gy_ref, gz_ref, state_ref, low_ref) = refs[
        10 + count :
    ]
    heads = cs_ref.shape[1]
    size = state_ref.shape[0]
    grad_low = grad_ref[...].astype(low)
    grad_low_ref[...] = grad_low
    step = grad_low.shape[1] // count
    grad_out = 0.0
    for r in range(count):
        grad_out = grad_out + dot(grad_low[:, r * step : (r + 1) * step], weights[r][...])
    norm_two = gate_norm(inner_total, squares_ref[...], squares_other_ref[...])
    branch = mine_ref[...].astype(wide) + other_ref[...].astype(wide)
    inner_dot = total_cols(grad_low.astype(wide) * branch)
    gate, y, gain = gate_ref[...], y_ref[...], gain_ref[...]
    sigmoid_value = jax.nn.sigmoid(gate)
    gate_act = gate * sigmoid_value
    product = y * gate_act
    normed = product * norm_two
    normed_out_ref[...] = (normed * gain).astype(low)
    gate_grad_ref[...] = total_rows(grad_out * normed)
    grad_product = norm_two * (grad_out * gain) - normed * (
        norm_two * norm_two * (inner_dot / inner_total)
    )
    gy = grad_product * gate_act
    gy_ref[...] = gy
    gz_ref[...] = (
        grad_product * y * (sigmoid_value * (1.0 + gate * (1.0 - sigmoid_value)))
    ).astype(low)
    table = heads_table(heads, inner)
    outputs = silu(lin_ref[:, inner + size :])
    state = dot(outputs, gy * to_channels(jnp.exp(cs_ref[...]), table), (0, 0))
    state_ref[...] = state
    low_ref[...] = state.astype(low)


def grads_body(count, rows_ref, values_ref, *outs):
    step = rows_ref.shape[1] // count
    for r in range(count):
        part = dot(rows_ref[:, r * step : (r + 1) * step], values_ref[...], (0, 0))
        outs[r][...] = part.astype(outs[r].dtype)


def intra_back_body(
    inner, gy_ref, lin_ref, dt_ref, cs_ref, cst_ref, carried_ref,
    gxw_ref, gb_ref, gc_ref, gcs_ref, rows_ref, cols_ref,
):
    length, mixed = lin_ref.shape
    size = (mixed - inner) // 2
    heads = dt_ref.shape[1]
    width = inner // heads
    table = heads_table(heads, inner)
    inputs = silu(lin_ref[:, inner : inner + size])
    outputs = silu(lin_ref[:, inner + size :])
    scores = dot(outputs, inputs, (1, 1))
    causal = triangle(length, False)
    weighted = (silu(lin_ref[:, :inner]) * to_channels(dt_ref[...], table)).astype(low)
    gy = gy_ref[...]
    rise = to_channels(jnp.exp(cs_ref[...]), table)
    lifted = gy * rise
    gc = dot(lifted, carried_ref[...], (1, 1))
    inter = to_heads(lifted * dot(outputs, carried_ref[...]), table)
    gy_low = gy.astype(low)
    lane = lax.broadcasted_iota(jnp.int32, (length, 2 * width), 1)
    head_lane = lax.broadcasted_iota(jnp.int32, (length, heads), 1)
    grad_scores = jnp.zeros((length, length), wide)
    for pair in range(heads // 2):
        columns = slice(pair * 2 * width, (pair + 1) * 2 * width)
        parts = []
        for half in (0, 1):
            head = 2 * pair + half
            mine = (lane < width) if half == 0 else (lane >= width)
            gaps = cs_ref[:, head : head + 1] - cst_ref[head : head + 1, :]
            decays = jnp.exp(jnp.where(causal, gaps, -1e30))
            mixing = scores * decays
            grad_mixing = dot(
                jnp.where(mine, gy[:, columns], 0.0), weighted[:, columns], (1, 1)
            )
            grad_scores = grad_scores + grad_mixing * decays
            through = grad_mixing * mixing
            inter = inter + jnp.where(head_lane == head, total_cols(through), 0.0)
            cols_ref[head : head + 1, :] = total_rows(through)
            parts.append(dot(mixing, gy_low[:, columns], (0, 0)))
        gxw_ref[:, columns] = jnp.where(lane < width, *parts)
    gcs_ref[...] = inter - cols_ref[...].T[:, :heads]
    gc_ref[...] = gc + dot(grad_scores, inputs)
    gb_ref[...] = dot(grad_scores, outputs, (0, 0))


def scan_back_body(
    inner, following_ref, carried_ref, gy_ref, gxw_ref, gb_ref, gc_ref, gcs_ref, lin_ref, conv_ref,
    edge_ref, dt_ref, cs_ref, step_ref, step_bias_ref, decay_ref, skip_ref, support_ref,
    glin_ref, gstep_ref, taps_grad_ref, bias_grad_ref, heads_ref, ext_ref,
):
    length, mixed = lin_ref.shape
    size = (mixed - inner) // 2
    heads = dt_ref.shape[1]
    table = heads_table(heads, inner)
    support = support_ref.shape[0]
    lin_x, lin_b, lin_c = lin_ref[:, :inner], lin_ref[:, inner : inner + size], lin_ref[:, inner + size :]
    x, inputs = silu(lin_x), silu(lin_b)
    dt, cs = dt_ref[...], cs_ref[...]
    last = cs[length - 1 :, :]
    tail = jnp.exp(last - cs)
    dt_x = to_channels(dt, table)
    tail_x = to_channels(tail, table)
    weighted = x * dt_x
    following = following_ref[...]
    along = tail_x * dot(inputs, following)
    gxw = gxw_ref[...] + along
    gb = gb_ref[...] + dot(weighted * tail_x, following, (1, 1))
    grad_tail = to_heads(weighted * along, table)
    block = jnp.broadcast_to(total_rows(following * carried_ref[...]), (8, inner))
    last_extra = total_rows(grad_tail) + to_heads(block, table)[:1] * jnp.exp(last)
    row = lax.broadcasted_iota(jnp.int32, (length, heads), 0)
    gcs = gcs_ref[...] - grad_tail + jnp.where(row == length - 1, last_extra, 0.0)
    ga = running(gcs, later=True)
    decay_rate = jnp.exp(decay_ref[...])
    gdt = to_heads(gxw * x, table) - ga * decay_rate
    gstep = gdt * jax.nn.sigmoid(step_ref[...] + step_bias_ref[...])
    gstep_ref[...] = gstep.astype(low)
    gy = gy_ref[...]
    skip_rows = jnp.broadcast_to(total_rows(gy * x), (8, inner))
    heads_ref[0:1, :] = total_rows(gstep)
    heads_ref[1:2, :] = -total_rows(ga * dt) * decay_rate
    heads_ref[2:3, :] = to_heads(skip_rows, table)[:1]
    heads_ref[3:, :] = jnp.zeros((5, heads), wide)
    skip_x = to_channels(skip_ref[...], table)[:1]
    glin_ref[:, :inner] = (skip_x * gy + gxw * dt_x) * silu_grad(lin_x)
    glin_ref[:, inner : inner + size] = gb * silu_grad(lin_b)
    glin_ref[:, inner + size :] = gc_ref[...] * silu_grad(lin_c)
    glin = glin_ref[...]
    ext_ref[:8] = edge_ref[...]
    ext_ref[8:] = conv_ref[...]
    for k in range(support):
        first = 9 - support + k
        taps_grad_ref[k : k + 1, :] = total_rows(ext_ref[first : first + length, :] * glin)
    bias_grad_ref[...] = total_rows(glin)


def enter_back_body(count, *refs):
    glin_ref, halo_ref, taps_ref, gstep_ref, gz_ref = refs[:5]
    scans, gates = refs[5 : 5 + count], refs[5 + count : 5 + 2 * count]
    gscan_ref, out_ref, ext_ref = refs[5 + 2 * count :]
    length, mixed = glin_ref.shape
    support = taps_ref.shape[0]
    ext_ref[:length] = glin_ref[...]
    ext_ref[length:] = halo_ref[...]
    grad = 0.0
    for k in range(support):
        first = support - 1 - k
        grad = grad + taps_ref[k : k + 1, :] * ext_ref[first : first + length, :]
    gscan_ref[:, :mixed] = grad.astype(low)
    gscan_ref[:, mixed:] = gstep_ref[...]
    gscan, gz = gscan_ref[...], gz_ref[...]
    step = out_ref.shape[1] // count
    for r in range(count):
        part = dot(gscan, scans[r][...], (1, 1)) + dot(gz, gates[r][...], (1, 1))
        out_ref[:, r * step : (r + 1) * step] = part.astype(low)


def norm_back_body(grad_ref, mine_ref, other_ref, hidden_ref, norm_ref, gain_ref, out_ref, prenorm_ref):
    grad_normed = mine_ref[...].astype(wide) + other_ref[...].astype(wide)
    hidden, norm_one = hidden_ref[...], norm_ref[...]
    unit = hidden * norm_one
    prenorm_ref[...] = total_rows(grad_normed * unit)
    scaled = grad_normed * gain_ref[...]
    mean = total_cols(scaled * hidden) / hidden.shape[1]
    out_ref[...] = grad_ref[...] + norm_one * scaled - unit * (norm_one * norm_one * mean)


def chained(decay, value, low_value, direction):
    count = lax.axis_size("context")
    carried = 0.0
    for step in range(count - 1):
        source = step if direction == 1 else count - 1 - step
        sent = (decay * carried + value).astype(low) if step else low_value
        carried = carried + lax.ppermute(
            sent, "context", [(source, source + direction)]
        ).astype(wide)
    return carried


def product_grads(rows, values):
    count = lax.axis_size("context")
    width = rows.shape[1] // count
    return call(
        functools.partial(grads_body, count),
        (rows, values),
        [((width, values.shape[1]), low if r & 1 else wide) for r in range(count)],
        flops=2 * rows.size * values.shape[1],
    )


def layer_forward(entry, weights, params):
    scan_weights, gate_weights, out_weights = weights
    (norm_scale, taps, tap_bias, step_bias, decay_log, skip_gain, gate_gain) = params
    count = lax.axis_size("context")
    length, width = entry[0].shape
    inner, mixed, heads = gate_gain.shape[1], taps.shape[1], decay_log.shape[1]
    size = (mixed - inner) // 2
    inner_total = inner * lax.axis_size("tensor")
    combine = len(entry) > 1
    results = [
        ((length, 1), wide), ((length, width), low), ((length, mixed), wide), ((length, heads), wide),
    ]
    norm_one, normed, conv_pre, step_pre, *rest = call(
        functools.partial(enter_body, count, inner_total, mixed, combine),
        (*entry, norm_scale, *scan_weights),
        results + [((length, width), wide)] * combine,
        flops=2 * length * width * mixed,
    )
    hidden_in = rest[0] if combine else entry[0]
    edge = shifted(conv_pre[length - 8 :], "context", 1)
    lin, dt, cs, cst, local_state, low_state, block_decay = call(
        functools.partial(states_body, inner),
        (conv_pre, edge, taps, tap_bias, step_pre, step_bias, decay_log),
        [
            ((length, mixed), wide), ((length, heads), wide), ((length, heads), wide),
            ((heads, length), wide), ((size, inner), wide), ((size, inner), low), ((1, inner), wide),
        ],
        [((length + 8, mixed), wide)],
        flops=4 * 10**9,
    )
    carried = chained(block_decay, local_state, low_state, 1)
    y_near, gate_pre = call(
        functools.partial(intra_body, inner, count),
        (lin, dt, cs, cst, skip_gain, normed, *gate_weights),
        [((length, inner), wide), ((length, inner), wide)],
        flops=8 * 10**9,
    )
    y, squares, mine = call(
        functools.partial(leave_body, inner, count),
        (lin, cs, y_near, carried, gate_pre, gate_gain, *out_weights),
        [((length, inner), wide), ((length, 1), wide), ((length, width), low)],
        flops=3 * 10**9,
    )
    squares_other = swapped(squares, "tensor", 1)
    other = swapped(mine, "tensor", 1)
    stored = (
        hidden_in, norm_one, normed, conv_pre, edge, step_pre, lin, dt, cs, cst, block_decay, carried,
        gate_pre, y, squares, squares_other, mine, other,
    )
    return (hidden_in, mine, other, squares, squares_other), stored


def layer_backward(gradient, weights, params, stored):
    scan_weights, gate_weights, out_weights = weights
    (norm_scale, taps, tap_bias, step_bias, decay_log, skip_gain, gate_gain) = params
    (
        hidden_in, norm_one, normed, conv_pre, edge, step_pre, lin, dt, cs, cst, block_decay, carried,
        gate_pre, y, squares, squares_other, mine, other,
    ) = stored
    count = lax.axis_size("context")
    length, width = gradient.shape
    inner, mixed, heads = gate_gain.shape[1], taps.shape[1], decay_log.shape[1]
    size = (mixed - inner) // 2
    inner_total = inner * lax.axis_size("tensor")
    grad_low, normed_out, gate_grad, gy, gz, grad_state, low_state = call(
        functools.partial(gate_back_body, inner, inner_total, count),
        (gradient, lin, cs, y, gate_pre, gate_gain, squares, squares_other, mine, other, *out_weights),
        [
            ((length, width), low), ((length, inner), low), ((1, inner), wide),
            ((length, inner), wide), ((length, inner), low), ((size, inner), wide), ((size, inner), low),
        ],
        flops=4 * 10**9,
    )
    following = chained(block_decay, grad_state, low_state, -1)
    outer_part = reduced(product_grads(grad_low, normed_out))
    gate_part = reduced(product_grads(normed, gz))
    gxw, gb, gc, gcs = call(
        functools.partial(intra_back_body, inner),
        (gy, lin, dt, cs, cst, carried),
        [((length, inner), wide), ((length, size), wide), ((length, size), wide), ((length, heads), wide)],
        [((8, 128), wide), ((max(128, heads), length), wide)],
        flops=12 * 10**9,
    )
    glin, gstep, taps_grad, tap_bias_grad, heads_grad = call(
        functools.partial(scan_back_body, inner),
        (
            following, carried, gy, gxw, gb, gc, gcs, lin, conv_pre, edge, dt, cs, step_pre, step_bias,
            decay_log, skip_gain, taps,
        ),
        [
            ((length, mixed), wide), ((length, heads), low), (taps.shape, wide), ((1, mixed), wide),
            ((8, heads), wide),
        ],
        [((length + 8, mixed), wide)],
        flops=6 * 10**9,
    )
    halo = shifted(glin[:8], "context", -1)
    gscan, mine_back = call(
        functools.partial(enter_back_body, count),
        (glin, halo, taps, gstep, gz, *scan_weights, *gate_weights),
        [((length, mixed + heads), low), ((length, width), low)],
        [((length + 8, mixed), wide)],
        flops=4 * 10**9,
    )
    other_back = swapped(mine_back, "tensor", 1)
    scan_part = reduced(product_grads(normed, gscan))
    grad_hidden, prenorm_grad = call(
        norm_back_body,
        (gradient, mine_back, other_back, hidden_in, norm_one, norm_scale),
        [((length, width), wide), ((1, width), wide)],
    )
    state_part = scan_part[:, inner:mixed]
    state_part = state_part.astype(wide) + swapped(state_part, "tensor", 1).astype(wide)
    large_part = (outer_part, gate_part, scan_part, state_part.astype(low))
    small_part = (
        from_local(prenorm_grad[0]),
        taps_grad[:, :inner],
        tap_bias_grad[0, :inner],
        taps_grad[:, inner:],
        tap_bias_grad[0, inner:],
        heads_grad[0],
        heads_grad[1],
        heads_grad[2],
        gate_grad[0],
    )
    return (grad_hidden, large_part, small_part)


def on_device(
    hidden,
    cotangent,
    norm_gain,
    inner_proj,
    state_proj,
    step_proj,
    inner_conv,
    inner_bias,
    state_conv,
    state_bias,
    step_bias,
    decay_log,
    skip_gain,
    gate_gain,
    out_proj,
):
    layers_here = inner_proj.shape[0]
    me, count = lax.axis_index("context"), lax.axis_size("context")
    rows = inner_proj.shape[1] // count

    def quarter(value, axis):
        return lax.dynamic_slice_in_dim(value, me * rows, rows, axis)

    inner_q, state_q, step_q = (quarter(v, 1) for v in (inner_proj, state_proj, step_proj))
    out_q = quarter(out_proj, 2)
    layer_weights = []
    for layer in range(layers_here):
        scan_q = jnp.concatenate([inner_q[layer, :, 1], state_q[layer], step_q[layer]], axis=1)
        rest_q = jnp.concatenate([inner_q[layer, :, 0], out_q[layer].T], axis=1)
        width = scan_q.shape[1]
        if layer == 0:
            scan_all, rest_all = gathered(scan_q), gathered(rest_q)
        else:
            both = gathered(jnp.concatenate([scan_q, rest_q], axis=1))
            scan_all, rest_all = both[:, :width], both[:, width:]
        inner = inner_proj.shape[3]
        layer_weights.append(
            (spread(scan_all), spread(rest_all[:, :inner]), spread(rest_all[:, inner:]))
        )
    taps = jnp.concatenate([inner_conv, state_conv], axis=-1)
    tap_bias = jnp.concatenate([inner_bias, state_bias], axis=-1)
    gains = to_local(norm_gain)
    entry = (to_local(hidden[0]).astype(wide),)
    kept_stored = []
    layer_params = []
    for layer in range(layers_here):
        layer_params.append(
            tuple(
                v[layer] if v.ndim == 3 else v[layer][None]
                for v in (gains, taps, tap_bias, step_bias, decay_log, skip_gain, gate_gain)
            )
        )
        entry, stored = layer_forward(entry, layer_weights[layer], layer_params[layer])
        kept_stored.append(stored)
    current, mine, other, squares, squares_other = entry
    norm_two = gate_norm(
        gate_gain.shape[1] * lax.axis_size("tensor"), squares, squares_other
    )
    current = current + norm_two * (mine.astype(wide) + other.astype(wide))
    output = from_local(current.astype(low))
    gradient = to_local(cotangent[0]).astype(wide)
    large_grads = [None] * layers_here
    small_grads = [None] * layers_here
    for layer in reversed(range(layers_here)):
        gradient, large_part, small_part = layer_backward(
            gradient, layer_weights[layer], layer_params[layer], kept_stored[layer]
        )
        state_small = everywhere(small_part[3:5], ("tensor",))
        small_grads[layer] = everywhere(
            small_part[:3] + tuple(state_small) + small_part[5:], ("context", "dp")
        )
        large_grads[layer] = [in_order(spread(part)).astype(wide) for part in large_part]
    summed = [jnp.stack([member[i] for member in small_grads]) for i in range(9)]
    inner = gate_gain.shape[1]
    mixed = taps.shape[-1]
    return (
        output[None],
        from_local(gradient.astype(low))[None],
        summed[0],
        jnp.stack([jnp.stack([m[1], m[2][:, :inner]], axis=1) for m in large_grads]),
        jnp.stack([m[3] for m in large_grads]),
        jnp.stack([m[2][:, mixed:] for m in large_grads]),
        summed[1],
        summed[2],
        summed[3],
        summed[4],
        summed[5],
        summed[6],
        summed[7],
        summed[8],
        jnp.stack([m[0].T for m in large_grads]),
    )


def solution(mesh):
    return jax.shard_map(
        on_device,
        mesh=mesh,
        in_specs=(
            P("dp", "context", None),
            P("dp", "context", None),
            P(),
            P(None, "dp", None, "tensor"),
            P(None, "dp", None),
            P(None, "dp", "tensor"),
            P(None, None, "tensor"),
            P(None, "tensor"),
            P(),
            P(),
            P(None, "tensor"),
            P(None, "tensor"),
            P(None, "tensor"),
            P(None, "tensor"),
            P(None, "tensor", "dp"),
        ),
        out_specs=(
            P("dp", "context", None),
            P("dp", "context", None),
            P(),
            P(None, "dp", None, "tensor"),
            P(None, "dp", None),
            P(None, "dp", "tensor"),
            P(None, None, "tensor"),
            P(None, "tensor"),
            P(),
            P(),
            P(None, "tensor"),
            P(None, "tensor"),
            P(None, "tensor"),
            P(None, "tensor"),
            P(None, "tensor", "dp"),
        ),
        check_vma=False,
    )
```

```python
import functools

import jax
import jax.numpy as jnp
from jax import lax
from jax.experimental import pallas as pl
from jax.experimental.pallas import tpu as pltpu
from jax.sharding import PartitionSpec as P

eps_norm = 1e-05
low = jnp.bfloat16
wide = jnp.float32


def swapped(value, axis, bit):
    return lax.ppermute(value, axis, [(i, i ^ bit) for i in range(lax.axis_size(axis))])


def shifted(value, axis, distance):
    count = lax.axis_size(axis)
    return lax.ppermute(
        value, axis, [(i, i + distance) for i in range(count) if 0 <= i + distance < count]
    )


def bits_of(axis):
    count = lax.axis_size(axis)
    assert count & (count - 1) == 0
    return [1 << k for k in range(count.bit_length() - 1)]


def spread(piece):
    pieces = {0: piece}
    for bit in reversed(bits_of("context")):
        for r in list(pieces):
            pieces[r | bit] = swapped(pieces[r], "context", bit)
    return [pieces[r] for r in range(len(pieces))]


def bit_order():
    order = [0]
    for bit in reversed(bits_of("context")):
        order = order + [r | bit for r in order]
    return order


def stacked_spread(piece):
    pieces = piece[None]
    for bit in reversed(bits_of("context")):
        pieces = jnp.concatenate([pieces, swapped(pieces, "context", bit)])
    return pieces


def halved_body(keep_ref, other_ref, keep_out_ref, send_ref):
    half = keep_ref.shape[0] // 2
    total = keep_ref[...].astype(wide) + other_ref[...].astype(wide)
    keep_out_ref[...] = total[:half]
    send_ref[...] = total[half:].astype(low)


def summed_body(keep_ref, other_ref, out_ref):
    out_ref[...] = (keep_ref[...].astype(wide) + other_ref[...].astype(wide)).astype(low)


def reduced(keep, send, after=()):
    bits = bits_of("context")
    for bit in bits:
        other = swapped(send, "context", bit)
        if bit == bits[-1]:
            total = call(summed_body, (keep, other), [(keep.shape, low)], after=after)[0]
        else:
            shape = (keep.shape[0] // 2, keep.shape[1])
            keep, send = call(halved_body, (keep, other), [(shape, wide), (shape, low)])
    mine = lax.psum_scatter(total, "dp", scatter_dimension=0, tiled=True)
    return total, mine, (send, stacked_spread)


def merged_body(cut, keep_ref, other_ref, out_ref):
    total = keep_ref[...].astype(wide) + other_ref[...].astype(wide)
    depth, width = total.shape
    total = jnp.swapaxes(total.reshape(cut + (width,)), 0, 1)
    out_ref[...] = total.reshape(depth, width).astype(low)


def reduced_late(keep, send):
    bits, shards = bits_of("context"), lax.axis_size("dp")
    kept = lax.axis_size("context") // 2
    other = swapped(send, "context", bits[0])
    cut = (kept, shards, keep.shape[0] // kept // shards)
    total = call(functools.partial(merged_body, cut), (keep, other), [(keep.shape, low)])[0]
    mine = lax.psum_scatter(total, "dp", scatter_dimension=0, tiled=True)

    def finished(mine):
        mine = mine.reshape(kept, -1, mine.shape[1])
        order = bit_order()[:kept]
        for bit in bits[1:]:
            other = swapped(mine, "context", bit)
            other = jnp.stack([other[order.index(r ^ bit)] for r in order])
            mine = (mine.astype(wide) + other.astype(wide)).astype(low)
        return mine

    return total, mine, finished


def gathered(piece, later=()):
    count, me = lax.axis_size("dp"), lax.axis_index("dp")
    if count > 4:
        return sum(later, lax.all_gather(piece, "dp", axis=0, tiled=True))
    ring = [(i, (i + 1) % count) for i in range(count)]
    held = [piece]
    for step in range(count - 1):
        held.append(lax.ppermute(held[-1], "dp", ring))
    stacked = jnp.stack(held)
    whole = jnp.concatenate(
        [lax.dynamic_index_in_dim(stacked, (me - j) % count, keepdims=False) for j in range(count)]
    )
    return sum(later, whole)


def everywhere(parts, axes):
    rows = -(-sum(part.size for part in parts) // 1024)
    flat = jnp.concatenate([part.reshape(-1) for part in parts])
    packed = jnp.pad(flat, (0, rows * 1024 - flat.size)).reshape(rows * 8, 128)
    for axis in axes:
        for bit in bits_of(axis):
            packed = packed + swapped(packed, axis, bit)
    flat = packed.reshape(-1)
    result, place = [], 0
    for part in parts:
        result.append(flat[place : place + part.size].reshape(part.shape))
        place += part.size
    return result


def to_local(value):
    me, count, shards = lax.axis_index("context"), lax.axis_size("context"), lax.axis_size("dp")
    lead = value.shape[:-1]
    cut = value.reshape(lead + (shards, count, -1))
    axis = len(lead) + 1
    return jnp.concatenate(
        [
            lax.dynamic_index_in_dim(cut, r ^ me, axis, keepdims=False).reshape(lead + (-1,))
            for r in range(count)
        ],
        axis=-1,
    )


def from_local(value):
    me, count, shards = lax.axis_index("context"), lax.axis_size("context"), lax.axis_size("dp")
    lead = value.shape[:-1]
    cut = value.reshape(lead + (count, shards, -1))
    axis = len(lead)
    return jnp.stack(
        [lax.dynamic_index_in_dim(cut, q ^ me, axis, keepdims=False) for q in range(count)],
        axis=axis + 1,
    ).reshape(value.shape)


def dot(left, right, contract=(1, 0)):
    return lax.dot_general(
        left.astype(low),
        right.astype(low),
        (((contract[0],), (contract[1],)), ((), ())),
        preferred_element_type=wide,
    )


def split(value, count):
    terms = []
    for _ in range(count):
        terms.append(value.astype(low))
        value = value - terms[-1].astype(wide)
    return terms


def triangle(length, later):
    row = lax.broadcasted_iota(jnp.int32, (length, length), 0)
    col = lax.broadcasted_iota(jnp.int32, (length, length), 1)
    return row <= col if later else row >= col


def running(value, later=False):
    table = jnp.where(triangle(value.shape[0], later), 1.0, 0.0)
    return sum(dot(table, term) for term in split(value, 3))


def running_t(value):
    table = jnp.where(triangle(value.shape[0], False), 1.0, 0.0)
    return sum(dot(term, table, (0, 1)) for term in split(value, 3))


def heads_table(heads, inner):
    row = lax.broadcasted_iota(jnp.int32, (heads, inner), 0)
    col = lax.broadcasted_iota(jnp.int32, (heads, inner), 1)
    width = inner // heads
    return jnp.where((col >= row * width) & (col < (row + 1) * width), 1.0, 0.0)


def to_channels(value, table):
    return sum(dot(term, table) for term in split(value, 2))


def to_heads(value, table):
    return sum(dot(term, table, (1, 1)) for term in split(value, 2))


def silu_grad(inputs):
    sigmoid_value = jax.nn.sigmoid(inputs)
    return sigmoid_value * (1.0 + inputs * (1.0 - sigmoid_value))


def silu(inputs):
    return inputs * jax.nn.sigmoid(inputs)


def softplus(inputs):
    return jnp.maximum(inputs, 0.0) + jnp.log1p(jnp.exp(-jnp.abs(inputs)))


def total_rows(value):
    return jnp.sum(value, axis=0, keepdims=True)


def total_cols(value):
    return jnp.sum(value, axis=1, keepdims=True)


def call(body, operands, results, scratch=(), flops=10**9, after=()):
    shapes = [jax.ShapeDtypeStruct(shape, kind) for shape, kind in results]
    size = sum(v.size * v.dtype.itemsize for v in list(operands) + shapes)
    first, rest = len(operands), len(operands) + len(after)
    return pl.pallas_call(
        lambda *refs: body(*refs[:first], *refs[rest:]),
        out_shape=shapes,
        in_specs=[pl.BlockSpec(memory_space=pltpu.VMEM)] * len(operands)
        + [pl.BlockSpec(memory_space=pl.ANY)] * len(after),
        scratch_shapes=[pltpu.VMEM(shape, kind) for shape, kind in scratch],
        compiler_params=pltpu.CompilerParams(vmem_limit_bytes=48 * 2**20),
        cost_estimate=pl.CostEstimate(flops=flops, bytes_accessed=size, transcendentals=0),
    )(*operands, *after)


def gate_norm(inner_total, squares, squares_other):
    return lax.rsqrt((squares + squares_other) / inner_total + eps_norm)


def weight(refs, order, r):
    if len(refs) == len(order):
        return refs[r]
    held, place = len(order) // len(refs), order.index(r)
    return refs[place // held].at[place % held]


def enter_body(order,  inner_total, mixed, combine, *refs):
    refs = list(refs)
    if combine:
        hidden_ref, mine_ref, other_ref, squares_ref, squares_other_ref = refs[:5]
        del refs[:5]
        norm_two = gate_norm(inner_total, squares_ref[...], squares_other_ref[...])
        branch = mine_ref[...].astype(wide) + other_ref[...].astype(wide)
        hidden = hidden_ref[...] + norm_two * branch
        refs[-1][...] = hidden
        del refs[-1]
    else:
        hidden = refs[0][...].astype(wide)
        del refs[0]
    gain_ref, weights, (norm_ref, normed_ref, conv_ref, step_ref) = refs[0], refs[1:-4], refs[-4:]
    norm_one = lax.rsqrt(
        total_cols(hidden * hidden) / hidden.shape[1] + eps_norm
    )
    normed = (hidden * norm_one * gain_ref[...]).astype(low)
    norm_ref[...] = norm_one
    normed_ref[...] = normed
    count = len(order)
    width = hidden.shape[1] // count
    total = 0.0
    for r in range(count):
        total = total + dot(
            normed[:, r * width : (r + 1) * width], weight(weights, order, r)[...]
        )
    conv_ref[...] = total[:, :mixed]
    step_ref[...] = total[:, mixed : mixed + step_ref.shape[1]]


def states_body(
    inner, conv_ref, edge_ref, taps_ref, bias_ref, step_ref, step_bias_ref, decay_ref,
    lin_ref, dt_ref, cs_ref, cst_ref, state_ref, low_ref, block_ref, ext_ref,
):
    length, mixed = conv_ref.shape
    size = (mixed - inner) // 2
    heads = step_ref.shape[1]
    ext_ref[:8] = edge_ref[...]
    ext_ref[8:] = conv_ref[...]
    support = taps_ref.shape[0]
    lin = bias_ref[...]
    for k in range(support):
        first = 9 - support + k
        lin = lin + taps_ref[k : k + 1, :] * ext_ref[first : first + length, :]
    lin_ref[...] = lin
    dt = softplus(step_ref[...] + step_bias_ref[...])
    rate = -dt * jnp.exp(decay_ref[...])
    cs = running(rate)
    last = cs[length - 1 :, :]
    dt_ref[...] = dt
    cs_ref[...] = cs
    cst_ref[...] = running_t(rate)
    table = heads_table(heads, inner)
    tailed = silu(lin[:, :inner]) * to_channels(dt * jnp.exp(last - cs), table)
    state = dot(silu(lin[:, inner : inner + size]), tailed, (0, 0))
    state_ref[...] = state
    low_ref[...] = state.astype(low)
    block_ref[...] = to_channels(jnp.broadcast_to(jnp.exp(last), (8, heads)), table)[:1]


def intra_body(inner, lin_ref, dt_ref, cs_ref, cst_ref, skip_ref, y_ref):
    length, mixed = lin_ref.shape
    size = (mixed - inner) // 2
    heads = dt_ref.shape[1]
    width = inner // heads
    table = heads_table(heads, inner)
    inputs = silu(lin_ref[:, inner : inner + size])
    outputs = silu(lin_ref[:, inner + size :])
    scores = dot(outputs, inputs, (1, 1))
    causal = triangle(length, False)
    x = silu(lin_ref[:, :inner])
    weighted = (x * to_channels(dt_ref[...], table)).astype(low)
    skipped = x * to_channels(skip_ref[...], table)[:1]
    lane = lax.broadcasted_iota(jnp.int32, (length, 2 * width), 1)
    for pair in range(heads // 2):
        columns = slice(pair * 2 * width, (pair + 1) * 2 * width)
        parts = []
        for head in (2 * pair, 2 * pair + 1):
            gaps = cs_ref[:, head : head + 1] - cst_ref[head : head + 1, :]
            mixing = scores * jnp.exp(jnp.where(causal, gaps, -1e30))
            parts.append(dot(mixing, weighted[:, columns]))
        y_ref[:, columns] = jnp.where(lane < width, *parts) + skipped[:, columns]


def leave_body(inner, count, *refs):
    lin_ref, cs_ref, y_ref, carried_ref, normed_ref, gain_ref = refs[:6]
    weights, (gate_ref, y_out_ref, squares_ref, out_ref) = refs[6:-4], refs[-4:]
    step = out_ref.shape[1] // count
    gate = 0.0
    for r in range(count):
        gate = gate + dot(normed_ref[:, r * step : (r + 1) * step], weights[r][:, :inner])
    gate_ref[...] = gate
    size = carried_ref.shape[0]
    heads = cs_ref.shape[1]
    table = heads_table(heads, inner)
    outputs = silu(lin_ref[:, inner + size :])
    rise = to_channels(jnp.exp(cs_ref[...]), table)
    y = y_ref[...] + rise * dot(outputs, carried_ref[...])
    y_out_ref[...] = y
    product = y * silu(gate)
    squares_ref[...] = total_cols(product * product)
    gained = (product * gain_ref[...]).astype(low)
    for r in range(count):
        out_ref[:, r * step : (r + 1) * step] = dot(gained, weights[r][:, inner:], (1, 1)).astype(low)


def gate_back_body(inner, inner_total, count, *refs):
    (grad_ref, lin_ref, cs_ref, y_ref, gate_ref, gain_ref, squares_ref, squares_other_ref,
     mine_ref, other_ref) = refs[:10]
    weights = refs[10 : 10 + count]
    (grad_low_ref, normed_out_ref, gate_grad_ref, gy_ref, gz_ref, state_ref, low_ref) = refs[
        10 + count :
    ]
    heads = cs_ref.shape[1]
    size = state_ref.shape[0]
    grad_low = grad_ref[...].astype(low)
    grad_low_ref[...] = grad_low
    step = grad_low.shape[1] // count
    grad_out = 0.0
    for r in range(count):
        grad_out = grad_out + dot(grad_low[:, r * step : (r + 1) * step], weights[r][:, inner:])
    norm_two = gate_norm(inner_total, squares_ref[...], squares_other_ref[...])
    branch = mine_ref[...].astype(wide) + other_ref[...].astype(wide)
    inner_dot = total_cols(grad_low.astype(wide) * branch)
    gate, y, gain = gate_ref[...], y_ref[...], gain_ref[...]
    sigmoid_value = jax.nn.sigmoid(gate)
    gate_act = gate * sigmoid_value
    product = y * gate_act
    normed = product * norm_two
    normed_out_ref[...] = (normed * gain).astype(low)
    gate_grad_ref[...] = total_rows(grad_out * normed)
    grad_product = norm_two * (grad_out * gain) - normed * (
        norm_two * norm_two * (inner_dot / inner_total)
    )
    gy = grad_product * gate_act
    gy_ref[...] = gy
    gz_ref[...] = (
        grad_product * y * (sigmoid_value * (1.0 + gate * (1.0 - sigmoid_value)))
    ).astype(low)
    table = heads_table(heads, inner)
    outputs = silu(lin_ref[:, inner + size :])
    state = dot(outputs, gy * to_channels(jnp.exp(cs_ref[...]), table), (0, 0))
    state_ref[...] = state
    low_ref[...] = state.astype(low)


def grads_body(order, pairs, *refs):
    keep_ref, send_ref = refs[-2:]
    count = len(order)
    column = 0
    for pair in range(pairs):
        rows_ref, values_ref = refs[2 * pair : 2 * pair + 2]
        step, width = rows_ref.shape[1] // count, values_ref.shape[1]
        for place, r in enumerate(order):
            out_ref = keep_ref if 2 * place < count else send_ref
            first = place % (count // 2) * step
            part = dot(rows_ref[:, r * step : (r + 1) * step], values_ref[...], (0, 0))
            out_ref[first : first + step, column : column + width] = part.astype(low)
        column += width


def intra_back_body(
    inner, gy_ref, lin_ref, dt_ref, cs_ref, cst_ref, carried_ref,
    gxw_ref, gb_ref, gc_ref, gcs_ref, rows_ref, cols_ref,
):
    length, mixed = lin_ref.shape
    size = (mixed - inner) // 2
    heads = dt_ref.shape[1]
    width = inner // heads
    table = heads_table(heads, inner)
    inputs = silu(lin_ref[:, inner : inner + size])
    outputs = silu(lin_ref[:, inner + size :])
    scores = dot(outputs, inputs, (1, 1))
    causal = triangle(length, False)
    weighted = (silu(lin_ref[:, :inner]) * to_channels(dt_ref[...], table)).astype(low)
    gy = gy_ref[...]
    rise = to_channels(jnp.exp(cs_ref[...]), table)
    lifted = gy * rise
    gc = dot(lifted, carried_ref[...], (1, 1))
    inter = to_heads(lifted * dot(outputs, carried_ref[...]), table)
    gy_low = gy.astype(low)
    lane = lax.broadcasted_iota(jnp.int32, (length, 2 * width), 1)
    head_lane = lax.broadcasted_iota(jnp.int32, (length, heads), 1)
    grad_scores = jnp.zeros((length, length), wide)
    for pair in range(heads // 2):
        columns = slice(pair * 2 * width, (pair + 1) * 2 * width)
        parts = []
        for half in (0, 1):
            head = 2 * pair + half
            mine = (lane < width) if half == 0 else (lane >= width)
            gaps = cs_ref[:, head : head + 1] - cst_ref[head : head + 1, :]
            decays = jnp.exp(jnp.where(causal, gaps, -1e30))
            mixing = scores * decays
            grad_mixing = dot(
                jnp.where(mine, gy[:, columns], 0.0), weighted[:, columns], (1, 1)
            )
            grad_scores = grad_scores + grad_mixing * decays
            through = grad_mixing * mixing
            inter = inter + jnp.where(head_lane == head, total_cols(through), 0.0)
            cols_ref[head : head + 1, :] = total_rows(through)
            parts.append(dot(mixing, gy_low[:, columns], (0, 0)))
        gxw_ref[:, columns] = jnp.where(lane < width, *parts)
    gcs_ref[...] = inter - cols_ref[...].T[:, :heads]
    gc_ref[...] = gc + dot(grad_scores, inputs)
    gb_ref[...] = dot(grad_scores, outputs, (0, 0))


def scan_back_body(
    inner, following_ref, carried_ref, gy_ref, gxw_ref, gb_ref, gc_ref, gcs_ref, lin_ref, conv_ref,
    edge_ref, dt_ref, cs_ref, step_ref, step_bias_ref, decay_ref, skip_ref, support_ref,
    glin_ref, gstep_ref, taps_grad_ref, bias_grad_ref, heads_ref, ext_ref,
):
    length, mixed = lin_ref.shape
    size = (mixed - inner) // 2
    heads = dt_ref.shape[1]
    table = heads_table(heads, inner)
    support = support_ref.shape[0]
    lin_x, lin_b, lin_c = lin_ref[:, :inner], lin_ref[:, inner : inner + size], lin_ref[:, inner + size :]
    x, inputs = silu(lin_x), silu(lin_b)
    dt, cs = dt_ref[...], cs_ref[...]
    last = cs[length - 1 :, :]
    tail = jnp.exp(last - cs)
    dt_x = to_channels(dt, table)
    tail_x = to_channels(tail, table)
    weighted = x * dt_x
    following = following_ref[...]
    along = tail_x * dot(inputs, following)
    gxw = gxw_ref[...] + along
    gb = gb_ref[...] + dot(weighted * tail_x, following, (1, 1))
    grad_tail = to_heads(weighted * along, table)
    block = jnp.broadcast_to(total_rows(following * carried_ref[...]), (8, inner))
    last_extra = total_rows(grad_tail) + to_heads(block, table)[:1] * jnp.exp(last)
    row = lax.broadcasted_iota(jnp.int32, (length, heads), 0)
    gcs = gcs_ref[...] - grad_tail + jnp.where(row == length - 1, last_extra, 0.0)
    ga = running(gcs, later=True)
    decay_rate = jnp.exp(decay_ref[...])
    gdt = to_heads(gxw * x, table) - ga * decay_rate
    gstep = gdt * jax.nn.sigmoid(step_ref[...] + step_bias_ref[...])
    gstep_ref[...] = gstep.astype(low)
    gy = gy_ref[...]
    skip_rows = jnp.broadcast_to(total_rows(gy * x), (8, inner))
    heads_ref[0:1, :] = total_rows(gstep)
    heads_ref[1:2, :] = -total_rows(ga * dt) * decay_rate
    heads_ref[2:3, :] = to_heads(skip_rows, table)[:1]
    heads_ref[3:, :] = jnp.zeros((5, heads), wide)
    skip_x = to_channels(skip_ref[...], table)[:1]
    glin_ref[:, :inner] = (skip_x * gy + gxw * dt_x) * silu_grad(lin_x)
    glin_ref[:, inner : inner + size] = gb * silu_grad(lin_b)
    glin_ref[:, inner + size :] = gc_ref[...] * silu_grad(lin_c)
    glin = glin_ref[...]
    ext_ref[:8] = edge_ref[...]
    ext_ref[8:] = conv_ref[...]
    for k in range(support):
        first = 9 - support + k
        taps_grad_ref[k : k + 1, :] = total_rows(ext_ref[first : first + length, :] * glin)
    bias_grad_ref[...] = total_rows(glin)


def enter_back_body(order, *refs):
    glin_ref, halo_ref, taps_ref, gstep_ref, *refs = refs
    gscan_ref, ext_ref = refs[-2:] if order is None else (refs[-3], refs[-1])
    length, mixed = glin_ref.shape
    support = taps_ref.shape[0]
    ext_ref[:length] = glin_ref[...]
    ext_ref[length:] = halo_ref[...]
    grad = 0.0
    for k in range(support):
        first = support - 1 - k
        grad = grad + taps_ref[k : k + 1, :] * ext_ref[first : first + length, :]
    heads = gstep_ref.shape[1]
    gscan_ref[:, :mixed] = grad.astype(low)
    gscan_ref[:, mixed:] = jnp.zeros((length, gscan_ref.shape[1] - mixed), low)
    gscan_ref[:, mixed : mixed + heads] = gstep_ref[...]
    if order is not None:
        width_body(order, gscan_ref, *refs[:-3], refs[-2])


def width_body(order, gscan_ref, gz_ref, *refs):
    count, out_ref = len(order), refs[-1]
    scans, gates = refs[:count], refs[count:-1]
    gscan, gz = gscan_ref[...], gz_ref[...]
    step = out_ref.shape[1] // count
    for r in range(count):
        part = dot(gscan, weight(scans, order, r)[...], (1, 1)) + dot(gz, gates[r][:, : gz.shape[1]], (1, 1))
        out_ref[:, r * step : (r + 1) * step] = part.astype(low)


def norm_back_body(grad_ref, mine_ref, other_ref, hidden_ref, norm_ref, gain_ref, out_ref, prenorm_ref):
    grad_normed = mine_ref[...].astype(wide) + other_ref[...].astype(wide)
    hidden, norm_one = hidden_ref[...], norm_ref[...]
    unit = hidden * norm_one
    prenorm_ref[...] = total_rows(grad_normed * unit)
    scaled = grad_normed * gain_ref[...]
    mean = total_cols(scaled * hidden) / hidden.shape[1]
    out_ref[...] = grad_ref[...] + norm_one * scaled - unit * (norm_one * norm_one * mean)


def joined_body(left_ref, right_ref, out_ref):
    width = left_ref.shape[1]
    out_ref[:, :width] = left_ref[...]
    out_ref[:, width:] = right_ref[...]


def finish_body(counts, order, inner, mixed, heads, me_ref, *refs):
    pieces = refs[: sum(counts)]
    inner_ref, state_ref, step_ref, outer_ref = refs[sum(counts) : sum(counts) + 4]
    outer_scratch = refs[-1]
    place = 0
    for layer, parts in enumerate(counts):
        for q in range(len(order)):
            rows = 0
            for index, r in enumerate(order):
                rows = jnp.where((q ^ me_ref[0]) == r, index, rows)
            columns = [pieces[place + index][rows].astype(wide) for index in range(parts)]
            value = jnp.concatenate(columns, axis=1) if len(columns) > 1 else columns[0]
            size = value.shape[0]
            here = slice(q * size, (q + 1) * size)
            outer_scratch[here, :] = value[:, :inner]
            inner_ref[layer, here, 0, :] = value[:, inner : 2 * inner]
            inner_ref[layer, here, 1, :] = value[:, 2 * inner : 3 * inner]
            state_ref[layer, here, :] = value[:, 3 * inner : 2 * inner + mixed]
            step_ref[layer, here, :] = value[:, 2 * inner + mixed : 2 * inner + mixed + heads]
        outer_ref[layer] = outer_scratch[...].T
        place += parts


def finish(layers, inner, mixed, heads):
    counts = [len(parts) for parts in layers]
    arrays = [array for parts in layers for array in parts]
    count, depth = len(layers), lax.axis_size("context") * arrays[0].shape[1]
    me = lax.axis_index("context").astype(jnp.int32)[None]
    shapes = [
        (count, depth, 2, inner), (count, depth, mixed - inner), (count, depth, heads),
        (count, inner, depth),
    ]
    return pl.pallas_call(
        functools.partial(finish_body, counts, bit_order(), inner, mixed, heads),
        out_shape=[jax.ShapeDtypeStruct(shape, wide) for shape in shapes],
        in_specs=[pl.BlockSpec(memory_space=pltpu.SMEM)]
        + [pl.BlockSpec(memory_space=pltpu.VMEM)] * len(arrays),
        scratch_shapes=[pltpu.VMEM((depth, inner), wide)],
        compiler_params=pltpu.CompilerParams(vmem_limit_bytes=48 * 2**20),
    )(me, *arrays)


def carry_body(decay_ref, value_ref, *refs):
    carried = sum(ref[...].astype(wide) for ref in refs[:-1])
    refs[-1][...] = (decay_ref[...] * carried + value_ref[...]).astype(low)


def chained(decay, value, low_value, direction, after=()):
    count = lax.axis_size("context")
    arrived = []
    for step in range(count - 1):
        source = step if direction == 1 else count - 1 - step
        sent = low_value
        if step:
            sent = call(carry_body, (decay, value, *arrived), [(value.shape, low)], after=after)[0]
        arrived.append(lax.ppermute(sent, "context", [(source, source + direction)]))
    return sum(part.astype(wide) for part in arrived)


def product_grads(*pairs, after=()):
    shape = (pairs[0][0].shape[1] // 2, sum(values.shape[1] for _, values in pairs))
    return call(
        functools.partial(grads_body, bit_order(), len(pairs)),
        [v for pair in pairs for v in pair],
        [(shape, low), (shape, low)],
        flops=2 * pairs[0][0].size * shape[1],
        after=after,
    )


def layer_forward(entry, weights, params):
    scan_weights, rest_weights = weights
    (norm_scale, taps, tap_bias, step_bias, decay_log, skip_gain, gate_gain) = params
    count = lax.axis_size("context")
    length, width = entry[0].shape
    inner, mixed, heads = gate_gain.shape[1], taps.shape[1], decay_log.shape[1]
    size = (mixed - inner) // 2
    inner_total = inner * lax.axis_size("tensor")
    combine = len(entry) > 1
    results = [
        ((length, 1), wide), ((length, width), low), ((length, mixed), wide), ((length, heads), wide),
    ]
    norm_one, normed, conv_pre, step_pre, *rest = call(
        functools.partial(enter_body, bit_order(), inner_total, mixed, combine),
        (*entry, norm_scale, *scan_weights),
        results + [((length, width), wide)] * combine,
        flops=2 * length * width * mixed,
    )
    hidden_in = rest[0] if combine else entry[0]
    edge = shifted(conv_pre[length - 8 :], "context", 1)
    lin, dt, cs, cst, local_state, low_state, block_decay = call(
        functools.partial(states_body, inner),
        (conv_pre, edge, taps, tap_bias, step_pre, step_bias, decay_log),
        [
            ((length, mixed), wide), ((length, heads), wide), ((length, heads), wide),
            ((heads, length), wide), ((size, inner), wide), ((size, inner), low), ((1, inner), wide),
        ],
        [((length + 8, mixed), wide)],
        flops=4 * 10**9,
    )
    y_near = call(
        functools.partial(intra_body, inner),
        (lin, dt, cs, cst, skip_gain),
        [((length, inner), wide)],
        flops=6 * 10**9,
    )[0]
    carried = chained(block_decay, local_state, low_state, 1, (y_near,))
    gate_pre, y, squares, mine = call(
        functools.partial(leave_body, inner, count),
        (lin, cs, y_near, carried, normed, gate_gain, *rest_weights),
        [
            ((length, inner), wide), ((length, inner), wide), ((length, 1), wide),
            ((length, width), low),
        ],
        flops=5 * 10**9,
    )
    squares_other = swapped(squares, "tensor", 1)
    other = swapped(mine, "tensor", 1)
    stored = (
        hidden_in, norm_one, normed, conv_pre, edge, step_pre, lin, dt, cs, cst, block_decay, carried,
        gate_pre, y, squares, squares_other, mine, other, y_near,
    )
    return (hidden_in, mine, other, squares, squares_other), stored


def layer_backward(gradient, weights, params, stored, last, after):
    scan_weights, rest_weights = weights
    (norm_scale, taps, tap_bias, step_bias, decay_log, skip_gain, gate_gain) = params
    (
        hidden_in, norm_one, normed, conv_pre, edge, step_pre, lin, dt, cs, cst, block_decay, carried,
        gate_pre, y, squares, squares_other, mine, other, _,
    ) = stored
    count = lax.axis_size("context")
    length, width = gradient.shape
    inner, mixed, heads = gate_gain.shape[1], taps.shape[1], decay_log.shape[1]
    size = (mixed - inner) // 2
    inner_total = inner * lax.axis_size("tensor")
    grad_low, normed_out, gate_grad, gy, gz, grad_state, low_state = call(
        functools.partial(gate_back_body, inner, inner_total, count),
        (gradient, lin, cs, y, gate_pre, gate_gain, squares, squares_other, mine, other, *rest_weights),
        [
            ((length, width), low), ((length, inner), low), ((1, inner), wide),
            ((length, inner), wide), ((length, inner), low), ((size, inner), wide), ((size, inner), low),
        ],
        flops=4 * 10**9,
        after=after[:1],
    )
    following = chained(block_decay, grad_state, low_state, -1)
    rest_total, rest_mine, rest_end = reduced_late(*product_grads((grad_low, normed_out), (normed, gz)))
    gxw, gb, gc, gcs = call(
        functools.partial(intra_back_body, inner),
        (gy, lin, dt, cs, cst, carried),
        [((length, inner), wide), ((length, size), wide), ((length, size), wide), ((length, heads), wide)],
        [((8, 128), wide), ((max(128, heads), length), wide)],
        flops=12 * 10**9,
    )
    glin, gstep, taps_grad, tap_bias_grad, heads_grad = call(
        functools.partial(scan_back_body, inner),
        (
            following, carried, gy, gxw, gb, gc, gcs, lin, conv_pre, edge, dt, cs, step_pre, step_bias,
            decay_log, skip_gain, taps,
        ),
        [
            ((length, mixed), wide), ((length, heads), low), (taps.shape, wide), ((1, mixed), wide),
            ((8, heads), wide),
        ],
        [((length + 8, mixed), wide)],
        flops=6 * 10**9,
        after=(rest_total,),
    )
    halo = shifted(glin[:8], "context", -1)
    width_operands = (gz, *scan_weights, *rest_weights)
    wide_shape = (length, scan_weights[0].shape[-1])
    enter_operands = (glin, halo, taps, gstep)
    enter_scratch = [((length + 8, mixed), wide)]
    if last:
        gscan = call(
            functools.partial(enter_back_body, None), enter_operands, [(wide_shape, low)], enter_scratch
        )[0]
        scan_cut = product_grads((normed, gscan))
        scan_total, scan_mine, scan_end = reduced(*scan_cut, after=(rest_mine,))
        sent, scan_end = scan_end
        mine_back = call(
            functools.partial(width_body, bit_order()),
            (gscan, *width_operands),
            [((length, width), low)],
            flops=4 * 10**9,
            after=(after[1], sent),
        )[0]
    else:
        gscan, mine_back = call(
            functools.partial(enter_back_body, bit_order()),
            enter_operands + width_operands,
            [(wide_shape, low), ((length, width), low)],
            enter_scratch,
            flops=4 * 10**9,
        )
    other_back = swapped(mine_back, "tensor", 1)
    if not last:
        scan_cut = product_grads((normed, gscan), after=(mine_back,))
        scan_total, scan_mine, scan_end = reduced_late(*scan_cut)
    grad_hidden, prenorm_grad = call(
        norm_back_body,
        (gradient, mine_back, other_back, hidden_in, norm_one, norm_scale),
        [((length, width), wide), ((1, width), wide)],
    )
    rest_part, scan_part = rest_mine, scan_mine
    state_part = scan_part[:, inner:mixed]
    state_part = state_part.astype(wide) + swapped(state_part, "tensor", 1).astype(wide)
    scan_part = jnp.concatenate(
        [scan_part[:, :inner], state_part.astype(low), scan_part[:, mixed:]], axis=1
    )
    if last:
        rest_part, scan_part = rest_end(rest_part), scan_end(scan_part)
        rest_part = jnp.concatenate([rest_part, swapped(rest_part, "context", 1)])
        large_part = (rest_part, scan_part)
    else:
        def large_part(after):
            shape = (rest_part.shape[0], rest_part.shape[1] + scan_part.shape[1])
            part = call(joined_body, (rest_part, scan_part), [(shape, low)], after=after)[0]
            part = rest_end(part)
            return (jnp.concatenate([part, swapped(part, "context", 1)]),)
    small_part = (
        prenorm_grad[0],
        taps_grad[:, :inner],
        tap_bias_grad[0, :inner],
        taps_grad[:, inner:],
        tap_bias_grad[0, inner:],
        heads_grad[0],
        heads_grad[1],
        heads_grad[2],
        gate_grad[0],
    )
    return (grad_hidden, large_part, small_part, (rest_mine, scan_mine, scan_total))


def on_device(
    hidden,
    cotangent,
    norm_gain,
    inner_proj,
    state_proj,
    step_proj,
    inner_conv,
    inner_bias,
    state_conv,
    state_bias,
    step_bias,
    decay_log,
    skip_gain,
    gate_gain,
    out_proj,
):
    layers_here = inner_proj.shape[0]
    me, count = lax.axis_index("context"), lax.axis_size("context")
    rows = inner_proj.shape[1] // count

    def quarter(value, axis):
        return lax.dynamic_slice_in_dim(value, me * rows, rows, axis)

    inner, heads = gate_gain.shape[1], decay_log.shape[1]
    mixed = inner + state_proj.shape[2]
    inner_q, state_q, step_q = (quarter(v, 1) for v in (inner_proj, state_proj, step_proj))
    step_q = jnp.pad(step_q, ((0, 0), (0, 0), (0, -(mixed + heads) % 128)))
    out_q = quarter(out_proj, 2)

    def own_rows(layer):
        scan = jnp.concatenate([inner_q[layer, :, 1], state_q[layer], step_q[layer]], axis=1)
        return scan, jnp.concatenate([inner_q[layer, :, 0], out_q[layer].T], axis=1)

    def token(value):
        return value[(slice(0, 1),) * value.ndim].reshape(1, 1).astype(low) * 0

    scan_own, rest_own = own_rows(0)
    scan_all = gathered(scan_own)
    layer_weights = [(spread(scan_all), spread(gathered(rest_own)))]

    def next_weights(layer, normed, near):
        scan, rest = own_rows(layer)
        scan = spread(gathered(scan + token(normed), (token(near),)))
        rest = lax.all_gather(rest + token(scan_all), "dp", axis=0, tiled=True)
        return scan, spread(rest + token(scan[count // 2]))

    taps = jnp.concatenate([inner_conv, state_conv], axis=-1)
    tap_bias = jnp.concatenate([inner_bias, state_bias], axis=-1)
    gains = to_local(norm_gain)
    entry = (to_local(hidden[0]).astype(wide),)
    kept_stored = []
    layer_params = []
    for layer in range(layers_here):
        layer_params.append(
            tuple(
                v[layer] if v.ndim == 3 else v[layer][None]
                for v in (gains, taps, tap_bias, step_bias, decay_log, skip_gain, gate_gain)
            )
        )
        entry, stored = layer_forward(entry, layer_weights[layer], layer_params[layer])
        kept_stored.append(stored)
        if layer + 1 < layers_here:
            layer_weights.append(next_weights(layer + 1, stored[2], stored[-1]))
    current, mine, other, squares, squares_other = entry
    norm_two = gate_norm(
        gate_gain.shape[1] * lax.axis_size("tensor"), squares, squares_other
    )
    current = current + norm_two * (mine.astype(wide) + other.astype(wide))
    output = from_local(current.astype(low))
    gradient = to_local(cotangent[0]).astype(wide)
    large_grads = [None] * layers_here
    after = ()
    small_grads = [None] * layers_here
    for layer in reversed(range(layers_here)):
        gradient, large_grads[layer], small_grads[layer], after = layer_backward(
            gradient, layer_weights[layer], layer_params[layer], kept_stored[layer], layer == 0, after
        )
    stacked = [jnp.stack([member[i] for member in small_grads]) for i in range(9)]
    stacked[0] = from_local(stacked[0])
    later = token(after[2]).astype(wide)[0, 0]
    stacked = [part + later for part in stacked]
    stacked[3:5] = everywhere(stacked[3:5], ("tensor",))
    summed = everywhere(stacked, ("context", "dp"))
    large_grads = [part(after[2:]) if callable(part) else part for part in large_grads]
    inner_grad, state_grad, step_grad, outer_grad = finish(large_grads, inner, mixed, heads)
    return (
        output[None],
        from_local(gradient.astype(low))[None],
        summed[0],
        inner_grad,
        state_grad,
        step_grad,
        summed[1],
        summed[2],
        summed[3],
        summed[4],
        summed[5],
        summed[6],
        summed[7],
        summed[8],
        outer_grad,
    )


def solution(mesh):
    return jax.shard_map(
        on_device,
        mesh=mesh,
        in_specs=(
            P("dp", "context", None),
            P("dp", "context", None),
            P(),
            P(None, "dp", None, "tensor"),
            P(None, "dp", None),
            P(None, "dp", "tensor"),
            P(None, None, "tensor"),
            P(None, "tensor"),
            P(),
            P(),
            P(None, "tensor"),
            P(None, "tensor"),
            P(None, "tensor"),
            P(None, "tensor"),
            P(None, "tensor", "dp"),
        ),
        out_specs=(
            P("dp", "context", None),
            P("dp", "context", None),
            P(),
            P(None, "dp", None, "tensor"),
            P(None, "dp", None),
            P(None, "dp", "tensor"),
            P(None, None, "tensor"),
            P(None, "tensor"),
            P(),
            P(),
            P(None, "tensor"),
            P(None, "tensor"),
            P(None, "tensor"),
            P(None, "tensor"),
            P(None, "tensor", "dp"),
        ),
        check_vma=False,
    )
```

```python
import functools

import jax
import jax.numpy as jnp
from jax import lax
from jax.experimental import pallas as pl
from jax.experimental.pallas import tpu as pltpu
from jax.sharding import PartitionSpec as P

eps_norm = 1e-05
low = jnp.bfloat16
wide = jnp.float32


def swapped(value, axis, bit):
    return lax.ppermute(value, axis, [(i, i ^ bit) for i in range(lax.axis_size(axis))])


def shifted(value, axis, distance):
    count = lax.axis_size(axis)
    return lax.ppermute(
        value, axis, [(i, i + distance) for i in range(count) if 0 <= i + distance < count]
    )


def bits_of(axis):
    count = lax.axis_size(axis)
    assert count & (count - 1) == 0
    return [1 << k for k in range(count.bit_length() - 1)]


def spread(piece):
    pieces = {0: piece}
    for bit in reversed(bits_of("context")):
        for r in list(pieces):
            pieces[r | bit] = swapped(pieces[r], "context", bit)
    return [pieces[r] for r in range(len(pieces))]


def bit_order():
    order = [0]
    for bit in reversed(bits_of("context")):
        order = order + [r | bit for r in order]
    return order


def stacked_spread(piece):
    pieces = piece[None]
    for bit in reversed(bits_of("context")):
        pieces = jnp.concatenate([pieces, swapped(pieces, "context", bit)])
    return pieces


def halved_body(keep_ref, other_ref, keep_out_ref, send_ref):
    half = keep_ref.shape[0] // 2
    total = keep_ref[...].astype(wide) + other_ref[...].astype(wide)
    keep_out_ref[...] = total[:half]
    send_ref[...] = total[half:].astype(low)


def summed_body(keep_ref, other_ref, out_ref):
    out_ref[...] = (keep_ref[...].astype(wide) + other_ref[...].astype(wide)).astype(low)


def reduced(keep, send, first_after=(), after=()):
    bits = bits_of("context")
    for bit in bits:
        other = swapped(send, "context", bit)
        if bit == bits[-1]:
            total = call(summed_body, (keep, other), [(keep.shape, low)], after=after)[0]
        else:
            shape = (keep.shape[0] // 2, keep.shape[1])
            keep, send = call(
                halved_body, (keep, other), [(shape, wide), (shape, low)], after=first_after
            )
    mine = lax.psum_scatter(total, "dp", scatter_dimension=0, tiled=True)
    return total, mine, (send, stacked_spread)


def merged_body(cut, keep_ref, other_ref, out_ref):
    total = keep_ref[...].astype(wide) + other_ref[...].astype(wide)
    depth, width = total.shape
    total = jnp.swapaxes(total.reshape(cut + (width,)), 0, 1)
    out_ref[...] = total.reshape(depth, width).astype(low)


def reduced_late(keep, send):
    bits, shards = bits_of("context"), lax.axis_size("dp")
    kept = lax.axis_size("context") // 2
    other = swapped(send, "context", bits[0])
    cut = (kept, shards, keep.shape[0] // kept // shards)
    total = call(functools.partial(merged_body, cut), (keep, other), [(keep.shape, low)])[0]
    mine = lax.psum_scatter(total, "dp", scatter_dimension=0, tiled=True)

    def finished(mine, later=0):
        mine = mine.reshape(kept, -1, mine.shape[1])
        order = bit_order()[:kept]
        for bit in bits[1:]:
            other = swapped(mine, "context", bit)
            other = jnp.stack([other[order.index(r ^ bit)] for r in order])
            mine = (mine.astype(wide) + other.astype(wide) + later).astype(low)
        return mine

    return total, mine, finished


def gathered(piece, later=()):
    count, me = lax.axis_size("dp"), lax.axis_index("dp")
    if count > 4:
        return sum(later, lax.all_gather(piece, "dp", axis=0, tiled=True))
    ring = [(i, (i + 1) % count) for i in range(count)]
    held = [piece]
    for step in range(count - 1):
        held.append(lax.ppermute(held[-1], "dp", ring))
    stacked = jnp.stack(held)
    whole = jnp.concatenate(
        [lax.dynamic_index_in_dim(stacked, (me - j) % count, keepdims=False) for j in range(count)]
    )
    return sum(later, whole)


def everywhere(parts, axes):
    rows = -(-sum(part.size for part in parts) // 1024)
    flat = jnp.concatenate([part.reshape(-1) for part in parts])
    packed = jnp.pad(flat, (0, rows * 1024 - flat.size)).reshape(rows * 8, 128)
    for axis in axes:
        for bit in bits_of(axis):
            packed = packed + swapped(packed, axis, bit)
    flat = packed.reshape(-1)
    result, place = [], 0
    for part in parts:
        result.append(flat[place : place + part.size].reshape(part.shape))
        place += part.size
    return result


def to_local(value):
    me, count, shards = lax.axis_index("context"), lax.axis_size("context"), lax.axis_size("dp")
    lead = value.shape[:-1]
    cut = value.reshape(lead + (shards, count, -1))
    axis = len(lead) + 1
    return jnp.concatenate(
        [
            lax.dynamic_index_in_dim(cut, r ^ me, axis, keepdims=False).reshape(lead + (-1,))
            for r in range(count)
        ],
        axis=-1,
    )


def from_local(value):
    me, count, shards = lax.axis_index("context"), lax.axis_size("context"), lax.axis_size("dp")
    lead = value.shape[:-1]
    cut = value.reshape(lead + (count, shards, -1))
    axis = len(lead)
    return jnp.stack(
        [lax.dynamic_index_in_dim(cut, q ^ me, axis, keepdims=False) for q in range(count)],
        axis=axis + 1,
    ).reshape(value.shape)


def dot(left, right, contract=(1, 0)):
    return lax.dot_general(
        left.astype(low),
        right.astype(low),
        (((contract[0],), (contract[1],)), ((), ())),
        preferred_element_type=wide,
    )


def split(value, count):
    terms = []
    for _ in range(count):
        terms.append(value.astype(low))
        value = value - terms[-1].astype(wide)
    return terms


def triangle(length, later):
    row = lax.broadcasted_iota(jnp.int32, (length, length), 0)
    col = lax.broadcasted_iota(jnp.int32, (length, length), 1)
    return row <= col if later else row >= col


def running(value, later=False):
    table = jnp.where(triangle(value.shape[0], later), 1.0, 0.0)
    return sum(dot(table, term) for term in split(value, 3))


def running_t(value):
    table = jnp.where(triangle(value.shape[0], False), 1.0, 0.0)
    return sum(dot(term, table, (0, 1)) for term in split(value, 3))


def heads_table(heads, inner):
    row = lax.broadcasted_iota(jnp.int32, (heads, inner), 0)
    col = lax.broadcasted_iota(jnp.int32, (heads, inner), 1)
    width = inner // heads
    return jnp.where((col >= row * width) & (col < (row + 1) * width), 1.0, 0.0)


def to_channels(value, table):
    return sum(dot(term, table) for term in split(value, 2))


def to_heads(value, table):
    return sum(dot(term, table, (1, 1)) for term in split(value, 2))


def silu_grad(inputs):
    sigmoid_value = jax.nn.sigmoid(inputs)
    return sigmoid_value * (1.0 + inputs * (1.0 - sigmoid_value))


def silu(inputs):
    return inputs * jax.nn.sigmoid(inputs)


def softplus(inputs):
    return jnp.maximum(inputs, 0.0) + jnp.log1p(jnp.exp(-jnp.abs(inputs)))


def total_rows(value):
    return jnp.sum(value, axis=0, keepdims=True)


def total_cols(value):
    return jnp.sum(value, axis=1, keepdims=True)


def call(body, operands, results, scratch=(), flops=10**9, after=()):
    shapes = [jax.ShapeDtypeStruct(shape, kind) for shape, kind in results]
    size = sum(v.size * v.dtype.itemsize for v in list(operands) + shapes)
    first, rest = len(operands), len(operands) + len(after)
    return pl.pallas_call(
        lambda *refs: body(*refs[:first], *refs[rest:]),
        out_shape=shapes,
        in_specs=[pl.BlockSpec(memory_space=pltpu.VMEM)] * len(operands)
        + [pl.BlockSpec(memory_space=pl.ANY)] * len(after),
        scratch_shapes=[pltpu.VMEM(shape, kind) for shape, kind in scratch],
        compiler_params=pltpu.CompilerParams(vmem_limit_bytes=48 * 2**20),
        cost_estimate=pl.CostEstimate(flops=flops, bytes_accessed=size, transcendentals=0),
    )(*operands, *after)


def gate_norm(inner_total, squares, squares_other):
    return lax.rsqrt((squares + squares_other) / inner_total + eps_norm)


def weight(refs, order, r):
    if len(refs) == len(order):
        return refs[r]
    held, place = len(order) // len(refs), order.index(r)
    return refs[place // held].at[place % held]


def enter_body(order,  inner_total, mixed, combine, *refs):
    refs = list(refs)
    if combine:
        hidden_ref, mine_ref, other_ref, squares_ref, squares_other_ref = refs[:5]
        del refs[:5]
        norm_two = gate_norm(inner_total, squares_ref[...], squares_other_ref[...])
        branch = mine_ref[...].astype(wide) + other_ref[...].astype(wide)
        hidden = hidden_ref[...] + norm_two * branch
        refs[-1][...] = hidden
        del refs[-1]
    else:
        hidden = refs[0][...].astype(wide)
        del refs[0]
    gain_ref, weights, (norm_ref, normed_ref, conv_ref, step_ref) = refs[0], refs[1:-4], refs[-4:]
    norm_one = lax.rsqrt(
        total_cols(hidden * hidden) / hidden.shape[1] + eps_norm
    )
    normed = (hidden * norm_one * gain_ref[...]).astype(low)
    norm_ref[...] = norm_one
    normed_ref[...] = normed
    count = len(order)
    width = hidden.shape[1] // count
    total = 0.0
    for r in range(count):
        total = total + dot(
            normed[:, r * width : (r + 1) * width], weight(weights, order, r)[...]
        )
    conv_ref[...] = total[:, :mixed]
    step_ref[...] = total[:, mixed : mixed + step_ref.shape[1]]


def states_body(
    inner, conv_ref, edge_ref, taps_ref, bias_ref, step_ref, step_bias_ref, decay_ref,
    lin_ref, dt_ref, cs_ref, cst_ref, state_ref, low_ref, block_ref, ext_ref,
):
    length, mixed = conv_ref.shape
    size = (mixed - inner) // 2
    heads = step_ref.shape[1]
    ext_ref[:8] = edge_ref[...]
    ext_ref[8:] = conv_ref[...]
    support = taps_ref.shape[0]
    lin = bias_ref[...]
    for k in range(support):
        first = 9 - support + k
        lin = lin + taps_ref[k : k + 1, :] * ext_ref[first : first + length, :]
    lin_ref[...] = lin
    dt = softplus(step_ref[...] + step_bias_ref[...])
    rate = -dt * jnp.exp(decay_ref[...])
    cs = running(rate)
    last = cs[length - 1 :, :]
    dt_ref[...] = dt
    cs_ref[...] = cs
    cst_ref[...] = running_t(rate)
    table = heads_table(heads, inner)
    tailed = silu(lin[:, :inner]) * to_channels(dt * jnp.exp(last - cs), table)
    state = dot(silu(lin[:, inner : inner + size]), tailed, (0, 0))
    state_ref[...] = state
    low_ref[...] = state.astype(low)
    block_ref[...] = to_channels(jnp.broadcast_to(jnp.exp(last), (8, heads)), table)[:1]


def intra_body(inner, lin_ref, dt_ref, cs_ref, cst_ref, skip_ref, y_ref):
    length, mixed = lin_ref.shape
    size = (mixed - inner) // 2
    heads = dt_ref.shape[1]
    width = inner // heads
    table = heads_table(heads, inner)
    inputs = silu(lin_ref[:, inner : inner + size])
    outputs = silu(lin_ref[:, inner + size :])
    scores = dot(outputs, inputs, (1, 1))
    causal = triangle(length, False)
    x = silu(lin_ref[:, :inner])
    weighted = (x * to_channels(dt_ref[...], table)).astype(low)
    skipped = x * to_channels(skip_ref[...], table)[:1]
    lane = lax.broadcasted_iota(jnp.int32, (length, 2 * width), 1)
    for pair in range(heads // 2):
        columns = slice(pair * 2 * width, (pair + 1) * 2 * width)
        parts = []
        for head in (2 * pair, 2 * pair + 1):
            gaps = cs_ref[:, head : head + 1] - cst_ref[head : head + 1, :]
            mixing = scores * jnp.exp(jnp.where(causal, gaps, -1e30))
            parts.append(dot(mixing, weighted[:, columns]))
        y_ref[:, columns] = jnp.where(lane < width, *parts) + skipped[:, columns]


def leave_body(inner, count, *refs):
    lin_ref, cs_ref, y_ref, carried_ref, normed_ref, gain_ref = refs[:6]
    weights, (gate_ref, y_out_ref, squares_ref, out_ref) = refs[6:-4], refs[-4:]
    step = out_ref.shape[1] // count
    gate = 0.0
    for r in range(count):
        gate = gate + dot(normed_ref[:, r * step : (r + 1) * step], weights[r][:, :inner])
    gate_ref[...] = gate
    size = carried_ref.shape[0]
    heads = cs_ref.shape[1]
    table = heads_table(heads, inner)
    outputs = silu(lin_ref[:, inner + size :])
    rise = to_channels(jnp.exp(cs_ref[...]), table)
    y = y_ref[...] + rise * dot(outputs, carried_ref[...])
    y_out_ref[...] = y
    product = y * silu(gate)
    squares_ref[...] = total_cols(product * product)
    gained = (product * gain_ref[...]).astype(low)
    for r in range(count):
        out_ref[:, r * step : (r + 1) * step] = dot(gained, weights[r][:, inner:], (1, 1)).astype(low)


def gate_back_body(inner, inner_total, count, *refs):
    (grad_ref, lin_ref, cs_ref, y_ref, gate_ref, gain_ref, squares_ref, squares_other_ref,
     mine_ref, other_ref) = refs[:10]
    weights = refs[10 : 10 + count]
    (grad_low_ref, normed_out_ref, gate_grad_ref, gy_ref, gz_ref, state_ref, low_ref) = refs[
        10 + count :
    ]
    heads = cs_ref.shape[1]
    size = state_ref.shape[0]
    grad_low = grad_ref[...].astype(low)
    grad_low_ref[...] = grad_low
    step = grad_low.shape[1] // count
    grad_out = 0.0
    for r in range(count):
        grad_out = grad_out + dot(grad_low[:, r * step : (r + 1) * step], weights[r][:, inner:])
    norm_two = gate_norm(inner_total, squares_ref[...], squares_other_ref[...])
    branch = mine_ref[...].astype(wide) + other_ref[...].astype(wide)
    inner_dot = total_cols(grad_low.astype(wide) * branch)
    gate, y, gain = gate_ref[...], y_ref[...], gain_ref[...]
    sigmoid_value = jax.nn.sigmoid(gate)
    gate_act = gate * sigmoid_value
    product = y * gate_act
    normed = product * norm_two
    normed_out_ref[...] = (normed * gain).astype(low)
    gate_grad_ref[...] = total_rows(grad_out * normed)
    grad_product = norm_two * (grad_out * gain) - normed * (
        norm_two * norm_two * (inner_dot / inner_total)
    )
    gy = grad_product * gate_act
    gy_ref[...] = gy
    gz_ref[...] = (
        grad_product * y * (sigmoid_value * (1.0 + gate * (1.0 - sigmoid_value)))
    ).astype(low)
    table = heads_table(heads, inner)
    outputs = silu(lin_ref[:, inner + size :])
    state = dot(outputs, gy * to_channels(jnp.exp(cs_ref[...]), table), (0, 0))
    state_ref[...] = state
    low_ref[...] = state.astype(low)


def grads_body(order, pairs, *refs):
    keep_ref, send_ref = refs[-2:]
    count = len(order)
    column = 0
    for pair in range(pairs):
        rows_ref, values_ref = refs[2 * pair : 2 * pair + 2]
        step, width = rows_ref.shape[1] // count, values_ref.shape[1]
        for place, r in enumerate(order):
            out_ref = keep_ref if 2 * place < count else send_ref
            first = place % (count // 2) * step
            part = dot(rows_ref[:, r * step : (r + 1) * step], values_ref[...], (0, 0))
            out_ref[first : first + step, column : column + width] = part.astype(low)
        column += width


def intra_back_body(
    inner, gy_ref, lin_ref, dt_ref, cs_ref, cst_ref, carried_ref,
    gxw_ref, gb_ref, gc_ref, gcs_ref, rows_ref, cols_ref,
):
    length, mixed = lin_ref.shape
    size = (mixed - inner) // 2
    heads = dt_ref.shape[1]
    width = inner // heads
    table = heads_table(heads, inner)
    inputs = silu(lin_ref[:, inner : inner + size])
    outputs = silu(lin_ref[:, inner + size :])
    scores = dot(outputs, inputs, (1, 1))
    causal = triangle(length, False)
    weighted = (silu(lin_ref[:, :inner]) * to_channels(dt_ref[...], table)).astype(low)
    gy = gy_ref[...]
    rise = to_channels(jnp.exp(cs_ref[...]), table)
    lifted = gy * rise
    gc = dot(lifted, carried_ref[...], (1, 1))
    inter = to_heads(lifted * dot(outputs, carried_ref[...]), table)
    gy_low = gy.astype(low)
    lane = lax.broadcasted_iota(jnp.int32, (length, 2 * width), 1)
    head_lane = lax.broadcasted_iota(jnp.int32, (length, heads), 1)
    grad_scores = jnp.zeros((length, length), wide)
    for pair in range(heads // 2):
        columns = slice(pair * 2 * width, (pair + 1) * 2 * width)
        parts = []
        for half in (0, 1):
            head = 2 * pair + half
            mine = (lane < width) if half == 0 else (lane >= width)
            gaps = cs_ref[:, head : head + 1] - cst_ref[head : head + 1, :]
            decays = jnp.exp(jnp.where(causal, gaps, -1e30))
            mixing = scores * decays
            grad_mixing = dot(
                jnp.where(mine, gy[:, columns], 0.0), weighted[:, columns], (1, 1)
            )
            grad_scores = grad_scores + grad_mixing * decays
            through = grad_mixing * mixing
            inter = inter + jnp.where(head_lane == head, total_cols(through), 0.0)
            cols_ref[head : head + 1, :] = total_rows(through)
            parts.append(dot(mixing, gy_low[:, columns], (0, 0)))
        gxw_ref[:, columns] = jnp.where(lane < width, *parts)
    gcs_ref[...] = inter - cols_ref[...].T[:, :heads]
    gc_ref[...] = gc + dot(grad_scores, inputs)
    gb_ref[...] = dot(grad_scores, outputs, (0, 0))


def scan_back_body(
    inner, following_ref, carried_ref, gy_ref, gxw_ref, gb_ref, gc_ref, gcs_ref, lin_ref, conv_ref,
    edge_ref, dt_ref, cs_ref, step_ref, step_bias_ref, decay_ref, skip_ref, support_ref,
    glin_ref, gstep_ref, taps_grad_ref, bias_grad_ref, heads_ref, ext_ref,
):
    length, mixed = lin_ref.shape
    size = (mixed - inner) // 2
    heads = dt_ref.shape[1]
    table = heads_table(heads, inner)
    support = support_ref.shape[0]
    lin_x, lin_b, lin_c = lin_ref[:, :inner], lin_ref[:, inner : inner + size], lin_ref[:, inner + size :]
    x, inputs = silu(lin_x), silu(lin_b)
    dt, cs = dt_ref[...], cs_ref[...]
    last = cs[length - 1 :, :]
    tail = jnp.exp(last - cs)
    dt_x = to_channels(dt, table)
    tail_x = to_channels(tail, table)
    weighted = x * dt_x
    following = following_ref[...]
    along = tail_x * dot(inputs, following)
    gxw = gxw_ref[...] + along
    gb = gb_ref[...] + dot(weighted * tail_x, following, (1, 1))
    grad_tail = to_heads(weighted * along, table)
    block = jnp.broadcast_to(total_rows(following * carried_ref[...]), (8, inner))
    last_extra = total_rows(grad_tail) + to_heads(block, table)[:1] * jnp.exp(last)
    row = lax.broadcasted_iota(jnp.int32, (length, heads), 0)
    gcs = gcs_ref[...] - grad_tail + jnp.where(row == length - 1, last_extra, 0.0)
    ga = running(gcs, later=True)
    decay_rate = jnp.exp(decay_ref[...])
    gdt = to_heads(gxw * x, table) - ga * decay_rate
    gstep = gdt * jax.nn.sigmoid(step_ref[...] + step_bias_ref[...])
    gstep_ref[...] = gstep.astype(low)
    gy = gy_ref[...]
    skip_rows = jnp.broadcast_to(total_rows(gy * x), (8, inner))
    heads_ref[0:1, :] = total_rows(gstep)
    heads_ref[1:2, :] = -total_rows(ga * dt) * decay_rate
    heads_ref[2:3, :] = to_heads(skip_rows, table)[:1]
    heads_ref[3:, :] = jnp.zeros((5, heads), wide)
    skip_x = to_channels(skip_ref[...], table)[:1]
    glin_ref[:, :inner] = (skip_x * gy + gxw * dt_x) * silu_grad(lin_x)
    glin_ref[:, inner : inner + size] = gb * silu_grad(lin_b)
    glin_ref[:, inner + size :] = gc_ref[...] * silu_grad(lin_c)
    glin = glin_ref[...]
    ext_ref[:8] = edge_ref[...]
    ext_ref[8:] = conv_ref[...]
    for k in range(support):
        first = 9 - support + k
        taps_grad_ref[k : k + 1, :] = total_rows(ext_ref[first : first + length, :] * glin)
    bias_grad_ref[...] = total_rows(glin)


def enter_back_body(order, *refs):
    glin_ref, halo_ref, taps_ref, gstep_ref, *refs = refs
    gscan_ref, ext_ref = refs[-2:] if order is None else (refs[-3], refs[-1])
    length, mixed = glin_ref.shape
    support = taps_ref.shape[0]
    ext_ref[:length] = glin_ref[...]
    ext_ref[length:] = halo_ref[...]
    grad = 0.0
    for k in range(support):
        first = support - 1 - k
        grad = grad + taps_ref[k : k + 1, :] * ext_ref[first : first + length, :]
    heads = gstep_ref.shape[1]
    gscan_ref[:, :mixed] = grad.astype(low)
    gscan_ref[:, mixed:] = jnp.zeros((length, gscan_ref.shape[1] - mixed), low)
    gscan_ref[:, mixed : mixed + heads] = gstep_ref[...]
    if order is not None:
        width_body(order, gscan_ref, *refs[:-3], refs[-2])


def width_body(order, gscan_ref, gz_ref, *refs):
    count, out_ref = len(order), refs[-1]
    scans, gates = refs[:count], refs[count:-1]
    gscan, gz = gscan_ref[...], gz_ref[...]
    step = out_ref.shape[1] // count
    for r in range(count):
        part = dot(gscan, weight(scans, order, r)[...], (1, 1)) + dot(gz, gates[r][:, : gz.shape[1]], (1, 1))
        out_ref[:, r * step : (r + 1) * step] = part.astype(low)


def norm_back_body(grad_ref, mine_ref, other_ref, hidden_ref, norm_ref, gain_ref, out_ref, prenorm_ref):
    grad_normed = mine_ref[...].astype(wide) + other_ref[...].astype(wide)
    hidden, norm_one = hidden_ref[...], norm_ref[...]
    unit = hidden * norm_one
    prenorm_ref[...] = total_rows(grad_normed * unit)
    scaled = grad_normed * gain_ref[...]
    mean = total_cols(scaled * hidden) / hidden.shape[1]
    out_ref[...] = grad_ref[...] + norm_one * scaled - unit * (norm_one * norm_one * mean)


def joined_body(left_ref, right_ref, out_ref):
    width = left_ref.shape[1]
    out_ref[:, :width] = left_ref[...]
    out_ref[:, width:] = right_ref[...]


def finish_body(counts, order, inner, mixed, heads, me_ref, *refs):
    pieces = refs[: sum(counts)]
    inner_ref, state_ref, step_ref, outer_ref = refs[sum(counts) : sum(counts) + 4]
    outer_scratch = refs[-1]
    place = 0
    for layer, parts in enumerate(counts):
        for q in range(len(order)):
            rows = 0
            for index, r in enumerate(order):
                rows = jnp.where((q ^ me_ref[0]) == r, index, rows)
            columns = [pieces[place + index][rows].astype(wide) for index in range(parts)]
            value = jnp.concatenate(columns, axis=1) if len(columns) > 1 else columns[0]
            size = value.shape[0]
            here = slice(q * size, (q + 1) * size)
            outer_scratch[here, :] = value[:, :inner]
            inner_ref[layer, here, 0, :] = value[:, inner : 2 * inner]
            inner_ref[layer, here, 1, :] = value[:, 2 * inner : 3 * inner]
            state_ref[layer, here, :] = value[:, 3 * inner : 2 * inner + mixed]
            step_ref[layer, here, :] = value[:, 2 * inner + mixed : 2 * inner + mixed + heads]
        outer_ref[layer] = outer_scratch[...].T
        place += parts


def finish(layers, inner, mixed, heads):
    counts = [len(parts) for parts in layers]
    arrays = [array for parts in layers for array in parts]
    count, depth = len(layers), lax.axis_size("context") * arrays[0].shape[1]
    me = lax.axis_index("context").astype(jnp.int32)[None]
    shapes = [
        (count, depth, 2, inner), (count, depth, mixed - inner), (count, depth, heads),
        (count, inner, depth),
    ]
    return pl.pallas_call(
        functools.partial(finish_body, counts, bit_order(), inner, mixed, heads),
        out_shape=[jax.ShapeDtypeStruct(shape, wide) for shape in shapes],
        in_specs=[pl.BlockSpec(memory_space=pltpu.SMEM)]
        + [pl.BlockSpec(memory_space=pltpu.VMEM)] * len(arrays),
        scratch_shapes=[pltpu.VMEM((depth, inner), wide)],
        compiler_params=pltpu.CompilerParams(vmem_limit_bytes=48 * 2**20),
    )(me, *arrays)


def carry_body(decay_ref, value_ref, *refs):
    carried = sum(ref[...].astype(wide) for ref in refs[:-1])
    refs[-1][...] = (decay_ref[...] * carried + value_ref[...]).astype(low)


def chained(decay, value, low_value, direction, after=()):
    count = lax.axis_size("context")
    arrived = []
    for step in range(count - 1):
        source = step if direction == 1 else count - 1 - step
        sent = low_value
        if step:
            sent = call(carry_body, (decay, value, *arrived), [(value.shape, low)], after=after)[0]
        arrived.append(lax.ppermute(sent, "context", [(source, source + direction)]))
    return sum(part.astype(wide) for part in arrived), sent


def product_grads(*pairs, after=()):
    shape = (pairs[0][0].shape[1] // 2, sum(values.shape[1] for _, values in pairs))
    return call(
        functools.partial(grads_body, bit_order(), len(pairs)),
        [v for pair in pairs for v in pair],
        [(shape, low), (shape, low)],
        flops=2 * pairs[0][0].size * shape[1],
        after=after,
    )


def layer_forward(entry, weights, params):
    scan_weights, rest_weights = weights
    (norm_scale, taps, tap_bias, step_bias, decay_log, skip_gain, gate_gain) = params
    count = lax.axis_size("context")
    length, width = entry[0].shape
    inner, mixed, heads = gate_gain.shape[1], taps.shape[1], decay_log.shape[1]
    size = (mixed - inner) // 2
    inner_total = inner * lax.axis_size("tensor")
    combine = len(entry) > 1
    results = [
        ((length, 1), wide), ((length, width), low), ((length, mixed), wide), ((length, heads), wide),
    ]
    norm_one, normed, conv_pre, step_pre, *rest = call(
        functools.partial(enter_body, bit_order(), inner_total, mixed, combine),
        (*entry, norm_scale, *scan_weights),
        results + [((length, width), wide)] * combine,
        flops=2 * length * width * mixed,
    )
    hidden_in = rest[0] if combine else entry[0]
    edge = shifted(conv_pre[length - 8 :], "context", 1)
    lin, dt, cs, cst, local_state, low_state, block_decay = call(
        functools.partial(states_body, inner),
        (conv_pre, edge, taps, tap_bias, step_pre, step_bias, decay_log),
        [
            ((length, mixed), wide), ((length, heads), wide), ((length, heads), wide),
            ((heads, length), wide), ((size, inner), wide), ((size, inner), low), ((1, inner), wide),
        ],
        [((length + 8, mixed), wide)],
        flops=4 * 10**9,
    )
    y_near = call(
        functools.partial(intra_body, inner),
        (lin, dt, cs, cst, skip_gain),
        [((length, inner), wide)],
        flops=6 * 10**9,
    )[0]
    carried, _ = chained(block_decay, local_state, low_state, 1, (y_near,))
    gate_pre, y, squares, mine = call(
        functools.partial(leave_body, inner, count),
        (lin, cs, y_near, carried, normed, gate_gain, *rest_weights),
        [
            ((length, inner), wide), ((length, inner), wide), ((length, 1), wide),
            ((length, width), low),
        ],
        flops=5 * 10**9,
    )
    squares_other = swapped(squares, "tensor", 1)
    other = swapped(mine, "tensor", 1)
    stored = (
        hidden_in, norm_one, normed, conv_pre, edge, step_pre, lin, dt, cs, cst, block_decay, carried,
        gate_pre, y, squares, squares_other, mine, other, y_near,
    )
    return (hidden_in, mine, other, squares, squares_other), stored


def layer_backward(gradient, weights, params, stored, last, after):
    scan_weights, rest_weights = weights
    (norm_scale, taps, tap_bias, step_bias, decay_log, skip_gain, gate_gain) = params
    (
        hidden_in, norm_one, normed, conv_pre, edge, step_pre, lin, dt, cs, cst, block_decay, carried,
        gate_pre, y, squares, squares_other, mine, other, _,
    ) = stored
    count = lax.axis_size("context")
    length, width = gradient.shape
    inner, mixed, heads = gate_gain.shape[1], taps.shape[1], decay_log.shape[1]
    size = (mixed - inner) // 2
    inner_total = inner * lax.axis_size("tensor")
    grad_low, normed_out, gate_grad, gy, gz, grad_state, low_state = call(
        functools.partial(gate_back_body, inner, inner_total, count),
        (gradient, lin, cs, y, gate_pre, gate_gain, squares, squares_other, mine, other, *rest_weights),
        [
            ((length, width), low), ((length, inner), low), ((1, inner), wide),
            ((length, inner), wide), ((length, inner), low), ((size, inner), wide), ((size, inner), low),
        ],
        flops=4 * 10**9,
        after=after[:1],
    )
    following, chain_end = chained(block_decay, grad_state, low_state, -1)
    rest_total, rest_mine, rest_end = reduced_late(*product_grads((grad_low, normed_out), (normed, gz)))
    gxw, gb, gc, gcs = call(
        functools.partial(intra_back_body, inner),
        (gy, lin, dt, cs, cst, carried),
        [((length, inner), wide), ((length, size), wide), ((length, size), wide), ((length, heads), wide)],
        [((8, 128), wide), ((max(128, heads), length), wide)],
        flops=12 * 10**9,
    )
    glin, gstep, taps_grad, tap_bias_grad, heads_grad = call(
        functools.partial(scan_back_body, inner),
        (
            following, carried, gy, gxw, gb, gc, gcs, lin, conv_pre, edge, dt, cs, step_pre, step_bias,
            decay_log, skip_gain, taps,
        ),
        [
            ((length, mixed), wide), ((length, heads), low), (taps.shape, wide), ((1, mixed), wide),
            ((8, heads), wide),
        ],
        [((length + 8, mixed), wide)],
        flops=6 * 10**9,
        after=(rest_total,),
    )
    halo = shifted(glin[:8], "context", -1)
    width_operands = (gz, *scan_weights, *rest_weights)
    wide_shape = (length, scan_weights[0].shape[-1])
    enter_operands = (glin, halo, taps, gstep)
    enter_scratch = [((length + 8, mixed), wide)]
    if last:
        gscan = call(
            functools.partial(enter_back_body, None), enter_operands, [(wide_shape, low)], enter_scratch
        )[0]
        scan_cut = product_grads((normed, gscan))
        mine_back = call(
            functools.partial(width_body, bit_order()),
            (gscan, *width_operands),
            [((length, width), low)],
            flops=4 * 10**9,
            after=(after[1], *scan_cut),
        )[0]
        scan_total, scan_mine, (_, scan_end) = reduced(
            *scan_cut, first_after=(mine_back,), after=(rest_mine,)
        )
    else:
        gscan, mine_back = call(
            functools.partial(enter_back_body, bit_order()),
            enter_operands + width_operands,
            [(wide_shape, low), ((length, width), low)],
            enter_scratch,
            flops=4 * 10**9,
        )
    other_back = swapped(mine_back, "tensor", 1)
    if not last:
        scan_cut = product_grads((normed, gscan), after=(mine_back,))
        scan_total, scan_mine, scan_end = reduced_late(*scan_cut)
    grad_hidden, prenorm_grad = call(
        norm_back_body,
        (gradient, mine_back, other_back, hidden_in, norm_one, norm_scale),
        [((length, width), wide), ((1, width), wide)],
        after=(scan_total,) if last else (),
    )
    def whole_states(part, first):
        here = part[..., first : first + mixed - inner]
        here = (here.astype(wide) + swapped(here, "tensor", 1).astype(wide)).astype(low)
        return jnp.concatenate(
            [part[..., :first], here, part[..., first + mixed - inner :]], axis=-1
        )

    if last:
        rest_part, scan_part = rest_end(rest_mine), scan_end(whole_states(scan_mine, inner))
        rest_part = jnp.concatenate([rest_part, swapped(rest_part, "context", 1)])
        large_part = (rest_part, scan_part)
    else:
        def large_part(after, later):
            shape = (rest_mine.shape[0], rest_mine.shape[1] + scan_mine.shape[1])
            part = call(joined_body, (rest_mine, scan_mine), [(shape, low)], after=after)[0]
            part = whole_states(rest_end(part, later), rest_mine.shape[1] + inner)
            return (jnp.concatenate([part, swapped(part, "context", 1)]),)
    small_part = (
        prenorm_grad[0],
        taps_grad[:, :inner],
        tap_bias_grad[0, :inner],
        taps_grad[:, inner:],
        tap_bias_grad[0, inner:],
        heads_grad[0],
        heads_grad[1],
        heads_grad[2],
        gate_grad[0],
    )
    return (grad_hidden, large_part, small_part, (rest_mine, scan_mine, scan_total, rest_total))


def on_device(
    hidden,
    cotangent,
    norm_gain,
    inner_proj,
    state_proj,
    step_proj,
    inner_conv,
    inner_bias,
    state_conv,
    state_bias,
    step_bias,
    decay_log,
    skip_gain,
    gate_gain,
    out_proj,
):
    layers_here = inner_proj.shape[0]
    me, count = lax.axis_index("context"), lax.axis_size("context")
    rows = inner_proj.shape[1] // count

    def quarter(value, axis):
        return lax.dynamic_slice_in_dim(value, me * rows, rows, axis)

    inner, heads = gate_gain.shape[1], decay_log.shape[1]
    mixed = inner + state_proj.shape[2]
    inner_q, state_q, step_q = (quarter(v, 1) for v in (inner_proj, state_proj, step_proj))
    step_q = jnp.pad(step_q, ((0, 0), (0, 0), (0, -(mixed + heads) % 128)))
    out_q = quarter(out_proj, 2)

    def own_rows(layer):
        scan = jnp.concatenate([inner_q[layer, :, 1], state_q[layer], step_q[layer]], axis=1)
        return scan, jnp.concatenate([inner_q[layer, :, 0], out_q[layer].T], axis=1)

    def token(value):
        return value[(slice(0, 1),) * value.ndim].reshape(1, 1).astype(low) * 0

    scan_own, rest_own = own_rows(0)
    scan_all = gathered(scan_own)
    layer_weights = [(spread(scan_all), spread(gathered(rest_own)))]

    def next_weights(layer, near):
        own = jnp.concatenate(own_rows(layer), axis=1) + token(scan_all)
        whole = lax.all_gather(own, "dp", axis=0, tiled=True)
        width = scan_all.shape[1]
        scan = spread(whole[:, :width] + token(near))
        return scan, spread(whole[:, width:] + token(scan[count // 2]))

    taps = jnp.concatenate([inner_conv, state_conv], axis=-1)
    tap_bias = jnp.concatenate([inner_bias, state_bias], axis=-1)
    gains = to_local(norm_gain)
    entry = (to_local(hidden[0]).astype(wide),)
    kept_stored = []
    layer_params = []
    for layer in range(layers_here):
        layer_params.append(
            tuple(
                v[layer] if v.ndim == 3 else v[layer][None]
                for v in (gains, taps, tap_bias, step_bias, decay_log, skip_gain, gate_gain)
            )
        )
        entry, stored = layer_forward(entry, layer_weights[layer], layer_params[layer])
        kept_stored.append(stored)
        if layer + 1 < layers_here:
            layer_weights.append(next_weights(layer + 1, stored[-1]))
    gradient = to_local(cotangent[0]).astype(wide)
    large_grads = [None] * layers_here
    after = ()
    small_grads = [None] * layers_here
    for layer in reversed(range(layers_here)):
        gradient, large_grads[layer], small_grads[layer], after = layer_backward(
            gradient, layer_weights[layer], layer_params[layer], kept_stored[layer], layer == 0, after
        )
    stacked = [jnp.stack([member[i] for member in small_grads]) for i in range(9)]
    stacked[0] = from_local(stacked[0])
    later = token(after[2]).astype(wide)[0, 0]
    stacked = [part + later for part in stacked]
    current, mine, other, squares, squares_other = entry
    norm_two = gate_norm(
        gate_gain.shape[1] * lax.axis_size("tensor"), squares + later, squares_other
    )
    current = current + norm_two * (mine.astype(wide) + other.astype(wide))
    output = from_local(current.astype(low))
    stacked[3:5] = everywhere(stacked[3:5], ("tensor",))
    summed = everywhere(stacked, ("dp", "context"))
    large_grads = [part(after[3:], later) if callable(part) else part for part in large_grads]
    inner_grad, state_grad, step_grad, outer_grad = finish(large_grads, inner, mixed, heads)
    return (
        output[None],
        from_local(gradient.astype(low))[None],
        summed[0],
        inner_grad,
        state_grad,
        step_grad,
        summed[1],
        summed[2],
        summed[3],
        summed[4],
        summed[5],
        summed[6],
        summed[7],
        summed[8],
        outer_grad,
    )


def solution(mesh):
    return jax.shard_map(
        on_device,
        mesh=mesh,
        in_specs=(
            P("dp", "context", None),
            P("dp", "context", None),
            P(),
            P(None, "dp", None, "tensor"),
            P(None, "dp", None),
            P(None, "dp", "tensor"),
            P(None, None, "tensor"),
            P(None, "tensor"),
            P(),
            P(),
            P(None, "tensor"),
            P(None, "tensor"),
            P(None, "tensor"),
            P(None, "tensor"),
            P(None, "tensor", "dp"),
        ),
        out_specs=(
            P("dp", "context", None),
            P("dp", "context", None),
            P(),
            P(None, "dp", None, "tensor"),
            P(None, "dp", None),
            P(None, "dp", "tensor"),
            P(None, None, "tensor"),
            P(None, "tensor"),
            P(),
            P(),
            P(None, "tensor"),
            P(None, "tensor"),
            P(None, "tensor"),
            P(None, "tensor"),
            P(None, "tensor", "dp"),
        ),
        check_vma=False,
    )
```

```python
import functools

import jax
import jax.numpy as jnp
from jax import lax
from jax.experimental import pallas as pl
from jax.experimental.pallas import tpu as pltpu
from jax.sharding import PartitionSpec as P

eps_norm = 1e-05
low = jnp.bfloat16
wide = jnp.float32


def swapped(value, axis, bit):
    return lax.ppermute(value, axis, [(i, i ^ bit) for i in range(lax.axis_size(axis))])


def shifted(value, axis, distance):
    count = lax.axis_size(axis)
    return lax.ppermute(
        value, axis, [(i, i + distance) for i in range(count) if 0 <= i + distance < count]
    )


def bits_of(axis):
    count = lax.axis_size(axis)
    assert count & (count - 1) == 0
    return [1 << k for k in range(count.bit_length() - 1)]


def spread(piece):
    pieces = {0: piece}
    for bit in reversed(bits_of("context")):
        for r in list(pieces):
            pieces[r | bit] = swapped(pieces[r], "context", bit)
    return [pieces[r] for r in range(len(pieces))]


def bit_order():
    order = [0]
    for bit in reversed(bits_of("context")):
        order = order + [r | bit for r in order]
    return order


def stacked_spread(piece):
    pieces = piece[None]
    for bit in reversed(bits_of("context")):
        pieces = jnp.concatenate([pieces, swapped(pieces, "context", bit)])
    return pieces


def halved_body(keep_ref, other_ref, keep_out_ref, send_ref):
    half = keep_ref.shape[0] // 2
    total = keep_ref[...].astype(wide) + other_ref[...].astype(wide)
    keep_out_ref[...] = total[:half]
    send_ref[...] = total[half:].astype(low)


def summed_body(keep_ref, other_ref, out_ref):
    out_ref[...] = (keep_ref[...].astype(wide) + other_ref[...].astype(wide)).astype(low)


def reduced(keep, send, first_after=(), after=()):
    bits = bits_of("context")
    for bit in bits:
        other = swapped(send, "context", bit)
        if bit == bits[-1]:
            total = call(summed_body, (keep, other), [(keep.shape, low)], after=after)[0]
        else:
            shape = (keep.shape[0] // 2, keep.shape[1])
            keep, send = call(
                halved_body, (keep, other), [(shape, wide), (shape, low)], after=first_after
            )
    mine = lax.psum_scatter(total, "dp", scatter_dimension=0, tiled=True)
    return total, mine, (send, stacked_spread)


def merged_body(cut, keep_ref, other_ref, out_ref):
    total = keep_ref[...].astype(wide) + other_ref[...].astype(wide)
    depth, width = total.shape
    total = jnp.swapaxes(total.reshape(cut + (width,)), 0, 1)
    out_ref[...] = total.reshape(depth, width).astype(low)


def reduced_late(keep, send):
    bits, shards = bits_of("context"), lax.axis_size("dp")
    kept = lax.axis_size("context") // 2
    other = swapped(send, "context", bits[0])
    cut = (kept, shards, keep.shape[0] // kept // shards)
    total = call(functools.partial(merged_body, cut), (keep, other), [(keep.shape, low)])[0]
    mine = lax.psum_scatter(total, "dp", scatter_dimension=0, tiled=True)

    def finished(mine, later=0):
        mine = mine.reshape(kept, -1, mine.shape[1])
        order = bit_order()[:kept]
        for bit in bits[1:]:
            other = swapped(mine, "context", bit)
            other = jnp.stack([other[order.index(r ^ bit)] for r in order])
            mine = (mine.astype(wide) + other.astype(wide) + later).astype(low)
        return mine

    return total, mine, finished


def gathered(piece, later=()):
    count, me = lax.axis_size("dp"), lax.axis_index("dp")
    if count > 4:
        return sum(later, lax.all_gather(piece, "dp", axis=0, tiled=True))
    ring = [(i, (i + 1) % count) for i in range(count)]
    held = [piece]
    for step in range(count - 1):
        held.append(lax.ppermute(held[-1], "dp", ring))
    stacked = jnp.stack(held)
    whole = jnp.concatenate(
        [lax.dynamic_index_in_dim(stacked, (me - j) % count, keepdims=False) for j in range(count)]
    )
    return sum(later, whole)


def everywhere(parts, axes):
    rows = -(-sum(part.size for part in parts) // 1024)
    flat = jnp.concatenate([part.reshape(-1) for part in parts])
    packed = jnp.pad(flat, (0, rows * 1024 - flat.size)).reshape(rows * 8, 128)
    for axis in axes:
        for bit in bits_of(axis):
            packed = packed + swapped(packed, axis, bit)
    flat = packed.reshape(-1)
    result, place = [], 0
    for part in parts:
        result.append(flat[place : place + part.size].reshape(part.shape))
        place += part.size
    return result


def to_local(value):
    me, count, shards = lax.axis_index("context"), lax.axis_size("context"), lax.axis_size("dp")
    lead = value.shape[:-1]
    cut = value.reshape(lead + (shards, count, -1))
    axis = len(lead) + 1
    return jnp.concatenate(
        [
            lax.dynamic_index_in_dim(cut, r ^ me, axis, keepdims=False).reshape(lead + (-1,))
            for r in range(count)
        ],
        axis=-1,
    )


def from_local(value):
    me, count, shards = lax.axis_index("context"), lax.axis_size("context"), lax.axis_size("dp")
    lead = value.shape[:-1]
    cut = value.reshape(lead + (count, shards, -1))
    axis = len(lead)
    return jnp.stack(
        [lax.dynamic_index_in_dim(cut, q ^ me, axis, keepdims=False) for q in range(count)],
        axis=axis + 1,
    ).reshape(value.shape)


def dot(left, right, contract=(1, 0)):
    return lax.dot_general(
        left.astype(low),
        right.astype(low),
        (((contract[0],), (contract[1],)), ((), ())),
        preferred_element_type=wide,
    )


def split(value, count):
    terms = []
    for _ in range(count):
        terms.append(value.astype(low))
        value = value - terms[-1].astype(wide)
    return terms


def triangle(length, later):
    row = lax.broadcasted_iota(jnp.int32, (length, length), 0)
    col = lax.broadcasted_iota(jnp.int32, (length, length), 1)
    return row <= col if later else row >= col


def running(value, later=False):
    table = jnp.where(triangle(value.shape[0], later), 1.0, 0.0)
    return sum(dot(table, term) for term in split(value, 3))


def running_t(value):
    table = jnp.where(triangle(value.shape[0], False), 1.0, 0.0)
    return sum(dot(term, table, (0, 1)) for term in split(value, 3))


def heads_table(heads, inner):
    row = lax.broadcasted_iota(jnp.int32, (heads, inner), 0)
    col = lax.broadcasted_iota(jnp.int32, (heads, inner), 1)
    width = inner // heads
    return jnp.where((col >= row * width) & (col < (row + 1) * width), 1.0, 0.0)


def to_channels(value, table):
    return sum(dot(term, table) for term in split(value, 2))


def to_heads(value, table):
    return sum(dot(term, table, (1, 1)) for term in split(value, 2))


def silu_grad(inputs):
    sigmoid_value = jax.nn.sigmoid(inputs)
    return sigmoid_value * (1.0 + inputs * (1.0 - sigmoid_value))


def silu(inputs):
    return inputs * jax.nn.sigmoid(inputs)


def softplus(inputs):
    return jnp.maximum(inputs, 0.0) + jnp.log1p(jnp.exp(-jnp.abs(inputs)))


def total_rows(value):
    return jnp.sum(value, axis=0, keepdims=True)


def total_cols(value):
    return jnp.sum(value, axis=1, keepdims=True)


def call(body, operands, results, scratch=(), flops=10**9, after=()):
    shapes = [jax.ShapeDtypeStruct(shape, kind) for shape, kind in results]
    size = sum(v.size * v.dtype.itemsize for v in list(operands) + shapes)
    first, rest = len(operands), len(operands) + len(after)
    return pl.pallas_call(
        lambda *refs: body(*refs[:first], *refs[rest:]),
        out_shape=shapes,
        in_specs=[pl.BlockSpec(memory_space=pltpu.VMEM)] * len(operands)
        + [pl.BlockSpec(memory_space=pl.ANY)] * len(after),
        scratch_shapes=[pltpu.VMEM(shape, kind) for shape, kind in scratch],
        compiler_params=pltpu.CompilerParams(vmem_limit_bytes=48 * 2**20),
        cost_estimate=pl.CostEstimate(flops=flops, bytes_accessed=size, transcendentals=0),
    )(*operands, *after)


def gate_norm(inner_total, squares, squares_other):
    return lax.rsqrt((squares + squares_other) / inner_total + eps_norm)


def weight(refs, order, r):
    if len(refs) == len(order):
        return refs[r]
    held, place = len(order) // len(refs), order.index(r)
    return refs[place // held].at[place % held]


def enter_body(order,  inner_total, mixed, combine, *refs):
    refs = list(refs)
    if combine:
        hidden_ref, mine_ref, other_ref, squares_ref, squares_other_ref = refs[:5]
        del refs[:5]
        norm_two = gate_norm(inner_total, squares_ref[...], squares_other_ref[...])
        branch = mine_ref[...].astype(wide) + other_ref[...].astype(wide)
        hidden = hidden_ref[...] + norm_two * branch
        refs[-1][...] = hidden
        del refs[-1]
    else:
        hidden = refs[0][...].astype(wide)
        del refs[0]
    gain_ref, weights, (norm_ref, normed_ref, conv_ref, step_ref) = refs[0], refs[1:-4], refs[-4:]
    norm_one = lax.rsqrt(
        total_cols(hidden * hidden) / hidden.shape[1] + eps_norm
    )
    normed = (hidden * norm_one * gain_ref[...]).astype(low)
    norm_ref[...] = norm_one
    normed_ref[...] = normed
    count = len(order)
    width = hidden.shape[1] // count
    total = 0.0
    for r in range(count):
        total = total + dot(
            normed[:, r * width : (r + 1) * width], weight(weights, order, r)[...]
        )
    conv_ref[...] = total[:, :mixed]
    step_ref[...] = total[:, mixed : mixed + step_ref.shape[1]]


def states_body(
    inner, conv_ref, edge_ref, taps_ref, bias_ref, step_ref, step_bias_ref, decay_ref,
    lin_ref, dt_ref, cs_ref, cst_ref, state_ref, low_ref, block_ref, ext_ref,
):
    length, mixed = conv_ref.shape
    size = (mixed - inner) // 2
    heads = step_ref.shape[1]
    ext_ref[:8] = edge_ref[...]
    ext_ref[8:] = conv_ref[...]
    support = taps_ref.shape[0]
    lin = bias_ref[...]
    for k in range(support):
        first = 9 - support + k
        lin = lin + taps_ref[k : k + 1, :] * ext_ref[first : first + length, :]
    lin_ref[...] = lin
    dt = softplus(step_ref[...] + step_bias_ref[...])
    rate = -dt * jnp.exp(decay_ref[...])
    cs = running(rate)
    last = cs[length - 1 :, :]
    dt_ref[...] = dt
    cs_ref[...] = cs
    cst_ref[...] = running_t(rate)
    table = heads_table(heads, inner)
    tailed = silu(lin[:, :inner]) * to_channels(dt * jnp.exp(last - cs), table)
    state = dot(silu(lin[:, inner : inner + size]), tailed, (0, 0))
    state_ref[...] = state
    low_ref[...] = state.astype(low)
    block_ref[...] = to_channels(jnp.broadcast_to(jnp.exp(last), (8, heads)), table)[:1]


def intra_body(inner, lin_ref, dt_ref, cs_ref, cst_ref, skip_ref, y_ref):
    length, mixed = lin_ref.shape
    size = (mixed - inner) // 2
    heads = dt_ref.shape[1]
    width = inner // heads
    table = heads_table(heads, inner)
    inputs = silu(lin_ref[:, inner : inner + size])
    outputs = silu(lin_ref[:, inner + size :])
    scores = dot(outputs, inputs, (1, 1))
    causal = triangle(length, False)
    x = silu(lin_ref[:, :inner])
    weighted = (x * to_channels(dt_ref[...], table)).astype(low)
    skipped = x * to_channels(skip_ref[...], table)[:1]
    lane = lax.broadcasted_iota(jnp.int32, (length, 2 * width), 1)
    for pair in range(heads // 2):
        columns = slice(pair * 2 * width, (pair + 1) * 2 * width)
        parts = []
        for head in (2 * pair, 2 * pair + 1):
            gaps = cs_ref[:, head : head + 1] - cst_ref[head : head + 1, :]
            mixing = scores * jnp.exp(jnp.where(causal, gaps, -1e30))
            parts.append(dot(mixing, weighted[:, columns]))
        y_ref[:, columns] = jnp.where(lane < width, *parts) + skipped[:, columns]


def leave_body(inner, count, *refs):
    lin_ref, cs_ref, y_ref, carried_ref, normed_ref, gain_ref = refs[:6]
    weights, (gate_ref, y_out_ref, squares_ref, out_ref) = refs[6:-4], refs[-4:]
    step = out_ref.shape[1] // count
    gate = 0.0
    for r in range(count):
        gate = gate + dot(normed_ref[:, r * step : (r + 1) * step], weights[r][:, :inner])
    gate_ref[...] = gate
    size = carried_ref.shape[0]
    heads = cs_ref.shape[1]
    table = heads_table(heads, inner)
    outputs = silu(lin_ref[:, inner + size :])
    rise = to_channels(jnp.exp(cs_ref[...]), table)
    y = y_ref[...] + rise * dot(outputs, carried_ref[...])
    y_out_ref[...] = y
    product = y * silu(gate)
    squares_ref[...] = total_cols(product * product)
    gained = (product * gain_ref[...]).astype(low)
    for r in range(count):
        out_ref[:, r * step : (r + 1) * step] = dot(gained, weights[r][:, inner:], (1, 1)).astype(low)


def gate_back_body(inner, inner_total, count, *refs):
    (grad_ref, lin_ref, cs_ref, y_ref, gate_ref, gain_ref, squares_ref, squares_other_ref,
     mine_ref, other_ref) = refs[:10]
    weights = refs[10 : 10 + count]
    (grad_low_ref, normed_out_ref, gate_grad_ref, gy_ref, gz_ref, state_ref, low_ref) = refs[
        10 + count :
    ]
    heads = cs_ref.shape[1]
    size = state_ref.shape[0]
    grad_low = grad_ref[...].astype(low)
    grad_low_ref[...] = grad_low
    step = grad_low.shape[1] // count
    grad_out = 0.0
    for r in range(count):
        grad_out = grad_out + dot(grad_low[:, r * step : (r + 1) * step], weights[r][:, inner:])
    norm_two = gate_norm(inner_total, squares_ref[...], squares_other_ref[...])
    branch = mine_ref[...].astype(wide) + other_ref[...].astype(wide)
    inner_dot = total_cols(grad_low.astype(wide) * branch)
    gate, y, gain = gate_ref[...], y_ref[...], gain_ref[...]
    sigmoid_value = jax.nn.sigmoid(gate)
    gate_act = gate * sigmoid_value
    product = y * gate_act
    normed = product * norm_two
    normed_out_ref[...] = (normed * gain).astype(low)
    gate_grad_ref[...] = total_rows(grad_out * normed)
    grad_product = norm_two * (grad_out * gain) - normed * (
        norm_two * norm_two * (inner_dot / inner_total)
    )
    gy = grad_product * gate_act
    gy_ref[...] = gy
    gz_ref[...] = (
        grad_product * y * (sigmoid_value * (1.0 + gate * (1.0 - sigmoid_value)))
    ).astype(low)
    table = heads_table(heads, inner)
    outputs = silu(lin_ref[:, inner + size :])
    state = dot(outputs, gy * to_channels(jnp.exp(cs_ref[...]), table), (0, 0))
    state_ref[...] = state
    low_ref[...] = state.astype(low)


def grads_body(order, pairs, *refs):
    keep_ref, send_ref = refs[-2:]
    count = len(order)
    column = 0
    for pair in range(pairs):
        rows_ref, values_ref = refs[2 * pair : 2 * pair + 2]
        step, width = rows_ref.shape[1] // count, values_ref.shape[1]
        for place, r in enumerate(order):
            out_ref = keep_ref if 2 * place < count else send_ref
            first = place % (count // 2) * step
            part = dot(rows_ref[:, r * step : (r + 1) * step], values_ref[...], (0, 0))
            out_ref[first : first + step, column : column + width] = part.astype(low)
        column += width


def intra_back_body(
    inner, gy_ref, lin_ref, dt_ref, cs_ref, cst_ref, carried_ref,
    gxw_ref, gb_ref, gc_ref, gcs_ref, rows_ref, cols_ref,
):
    length, mixed = lin_ref.shape
    size = (mixed - inner) // 2
    heads = dt_ref.shape[1]
    width = inner // heads
    table = heads_table(heads, inner)
    inputs = silu(lin_ref[:, inner : inner + size])
    outputs = silu(lin_ref[:, inner + size :])
    scores = dot(outputs, inputs, (1, 1))
    causal = triangle(length, False)
    weighted = (silu(lin_ref[:, :inner]) * to_channels(dt_ref[...], table)).astype(low)
    gy = gy_ref[...]
    rise = to_channels(jnp.exp(cs_ref[...]), table)
    lifted = gy * rise
    gc = dot(lifted, carried_ref[...], (1, 1))
    inter = to_heads(lifted * dot(outputs, carried_ref[...]), table)
    gy_low = gy.astype(low)
    lane = lax.broadcasted_iota(jnp.int32, (length, 2 * width), 1)
    head_lane = lax.broadcasted_iota(jnp.int32, (length, heads), 1)
    grad_scores = jnp.zeros((length, length), wide)
    for pair in range(heads // 2):
        columns = slice(pair * 2 * width, (pair + 1) * 2 * width)
        parts = []
        for half in (0, 1):
            head = 2 * pair + half
            mine = (lane < width) if half == 0 else (lane >= width)
            gaps = cs_ref[:, head : head + 1] - cst_ref[head : head + 1, :]
            decays = jnp.exp(jnp.where(causal, gaps, -1e30))
            mixing = scores * decays
            grad_mixing = dot(
                jnp.where(mine, gy[:, columns], 0.0), weighted[:, columns], (1, 1)
            )
            grad_scores = grad_scores + grad_mixing * decays
            through = grad_mixing * mixing
            inter = inter + jnp.where(head_lane == head, total_cols(through), 0.0)
            cols_ref[head : head + 1, :] = total_rows(through)
            parts.append(dot(mixing, gy_low[:, columns], (0, 0)))
        gxw_ref[:, columns] = jnp.where(lane < width, *parts)
    gcs_ref[...] = inter - cols_ref[...].T[:, :heads]
    gc_ref[...] = gc + dot(grad_scores, inputs)
    gb_ref[...] = dot(grad_scores, outputs, (0, 0))


def scan_back_body(
    inner, following_ref, carried_ref, gy_ref, gxw_ref, gb_ref, gc_ref, gcs_ref, lin_ref, conv_ref,
    edge_ref, dt_ref, cs_ref, step_ref, step_bias_ref, decay_ref, skip_ref, support_ref,
    glin_ref, gstep_ref, taps_grad_ref, bias_grad_ref, heads_ref, ext_ref,
):
    length, mixed = lin_ref.shape
    size = (mixed - inner) // 2
    heads = dt_ref.shape[1]
    table = heads_table(heads, inner)
    support = support_ref.shape[0]
    lin_x, lin_b, lin_c = lin_ref[:, :inner], lin_ref[:, inner : inner + size], lin_ref[:, inner + size :]
    x, inputs = silu(lin_x), silu(lin_b)
    dt, cs = dt_ref[...], cs_ref[...]
    last = cs[length - 1 :, :]
    tail = jnp.exp(last - cs)
    dt_x = to_channels(dt, table)
    tail_x = to_channels(tail, table)
    weighted = x * dt_x
    following = following_ref[...]
    along = tail_x * dot(inputs, following)
    gxw = gxw_ref[...] + along
    gb = gb_ref[...] + dot(weighted * tail_x, following, (1, 1))
    grad_tail = to_heads(weighted * along, table)
    block = jnp.broadcast_to(total_rows(following * carried_ref[...]), (8, inner))
    last_extra = total_rows(grad_tail) + to_heads(block, table)[:1] * jnp.exp(last)
    row = lax.broadcasted_iota(jnp.int32, (length, heads), 0)
    gcs = gcs_ref[...] - grad_tail + jnp.where(row == length - 1, last_extra, 0.0)
    ga = running(gcs, later=True)
    decay_rate = jnp.exp(decay_ref[...])
    gdt = to_heads(gxw * x, table) - ga * decay_rate
    gstep = gdt * jax.nn.sigmoid(step_ref[...] + step_bias_ref[...])
    gstep_ref[...] = gstep.astype(low)
    gy = gy_ref[...]
    skip_rows = jnp.broadcast_to(total_rows(gy * x), (8, inner))
    heads_ref[0:1, :] = total_rows(gstep)
    heads_ref[1:2, :] = -total_rows(ga * dt) * decay_rate
    heads_ref[2:3, :] = to_heads(skip_rows, table)[:1]
    heads_ref[3:, :] = jnp.zeros((5, heads), wide)
    skip_x = to_channels(skip_ref[...], table)[:1]
    glin_ref[:, :inner] = (skip_x * gy + gxw * dt_x) * silu_grad(lin_x)
    glin_ref[:, inner : inner + size] = gb * silu_grad(lin_b)
    glin_ref[:, inner + size :] = gc_ref[...] * silu_grad(lin_c)
    glin = glin_ref[...]
    ext_ref[:8] = edge_ref[...]
    ext_ref[8:] = conv_ref[...]
    for k in range(support):
        first = 9 - support + k
        taps_grad_ref[k : k + 1, :] = total_rows(ext_ref[first : first + length, :] * glin)
    bias_grad_ref[...] = total_rows(glin)


def enter_back_body(order, *refs):
    glin_ref, halo_ref, taps_ref, gstep_ref, *refs = refs
    gscan_ref, ext_ref = refs[-2:] if order is None else (refs[-3], refs[-1])
    length, mixed = glin_ref.shape
    support = taps_ref.shape[0]
    ext_ref[:length] = glin_ref[...]
    ext_ref[length:] = halo_ref[...]
    grad = 0.0
    for k in range(support):
        first = support - 1 - k
        grad = grad + taps_ref[k : k + 1, :] * ext_ref[first : first + length, :]
    heads = gstep_ref.shape[1]
    gscan_ref[:, :mixed] = grad.astype(low)
    gscan_ref[:, mixed:] = jnp.zeros((length, gscan_ref.shape[1] - mixed), low)
    gscan_ref[:, mixed : mixed + heads] = gstep_ref[...]
    if order is not None:
        width_body(order, gscan_ref, *refs[:-3], refs[-2])


def width_body(order, gscan_ref, gz_ref, *refs):
    count, out_ref = len(order), refs[-1]
    scans, gates = refs[:count], refs[count:-1]
    gscan, gz = gscan_ref[...], gz_ref[...]
    step = out_ref.shape[1] // count
    for r in range(count):
        part = dot(gscan, weight(scans, order, r)[...], (1, 1)) + dot(gz, gates[r][:, : gz.shape[1]], (1, 1))
        out_ref[:, r * step : (r + 1) * step] = part.astype(low)


def norm_back_body(grad_ref, mine_ref, other_ref, hidden_ref, norm_ref, gain_ref, out_ref, prenorm_ref):
    grad_normed = mine_ref[...].astype(wide) + other_ref[...].astype(wide)
    hidden, norm_one = hidden_ref[...], norm_ref[...]
    unit = hidden * norm_one
    prenorm_ref[...] = total_rows(grad_normed * unit)
    scaled = grad_normed * gain_ref[...]
    mean = total_cols(scaled * hidden) / hidden.shape[1]
    out_ref[...] = grad_ref[...] + norm_one * scaled - unit * (norm_one * norm_one * mean)


def joined_body(left_ref, right_ref, out_ref):
    width = left_ref.shape[1]
    out_ref[:, :width] = left_ref[...]
    out_ref[:, width:] = right_ref[...]


def finish_body(counts, order, inner, mixed, heads, me_ref, *refs):
    pieces = refs[: sum(counts)]
    inner_ref, state_ref, step_ref, outer_ref = refs[sum(counts) : sum(counts) + 4]
    outer_scratch = refs[-1]
    place = 0
    for layer, parts in enumerate(counts):
        for q in range(len(order)):
            rows = 0
            for index, r in enumerate(order):
                rows = jnp.where((q ^ me_ref[0]) == r, index, rows)
            columns = [pieces[place + index][rows].astype(wide) for index in range(parts)]
            value = jnp.concatenate(columns, axis=1) if len(columns) > 1 else columns[0]
            size = value.shape[0]
            here = slice(q * size, (q + 1) * size)
            outer_scratch[here, :] = value[:, :inner]
            inner_ref[layer, here, 0, :] = value[:, inner : 2 * inner]
            inner_ref[layer, here, 1, :] = value[:, 2 * inner : 3 * inner]
            state_ref[layer, here, :] = value[:, 3 * inner : 2 * inner + mixed]
            step_ref[layer, here, :] = value[:, 2 * inner + mixed : 2 * inner + mixed + heads]
        outer_ref[layer] = outer_scratch[...].T
        place += parts


def finish(layers, inner, mixed, heads):
    counts = [len(parts) for parts in layers]
    arrays = [array for parts in layers for array in parts]
    count, depth = len(layers), lax.axis_size("context") * arrays[0].shape[1]
    me = lax.axis_index("context").astype(jnp.int32)[None]
    shapes = [
        (count, depth, 2, inner), (count, depth, mixed - inner), (count, depth, heads),
        (count, inner, depth),
    ]
    return pl.pallas_call(
        functools.partial(finish_body, counts, bit_order(), inner, mixed, heads),
        out_shape=[jax.ShapeDtypeStruct(shape, wide) for shape in shapes],
        in_specs=[pl.BlockSpec(memory_space=pltpu.SMEM)]
        + [pl.BlockSpec(memory_space=pltpu.VMEM)] * len(arrays),
        scratch_shapes=[pltpu.VMEM((depth, inner), wide)],
        compiler_params=pltpu.CompilerParams(vmem_limit_bytes=48 * 2**20),
    )(me, *arrays)


def carry_body(decay_ref, value_ref, *refs):
    carried = sum(ref[...].astype(wide) for ref in refs[:-1])
    refs[-1][...] = (decay_ref[...] * carried + value_ref[...]).astype(low)


def chained(decay, value, low_value, direction, after=()):
    count = lax.axis_size("context")
    arrived = []
    for step in range(count - 1):
        source = step if direction == 1 else count - 1 - step
        sent = low_value
        if step:
            sent = call(carry_body, (decay, value, *arrived), [(value.shape, low)], after=after)[0]
        arrived.append(lax.ppermute(sent, "context", [(source, source + direction)]))
    return sum(part.astype(wide) for part in arrived), sent


def product_grads(*pairs, after=()):
    shape = (pairs[0][0].shape[1] // 2, sum(values.shape[1] for _, values in pairs))
    return call(
        functools.partial(grads_body, bit_order(), len(pairs)),
        [v for pair in pairs for v in pair],
        [(shape, low), (shape, low)],
        flops=2 * pairs[0][0].size * shape[1],
        after=after,
    )


def layer_forward(entry, weights, params, begin):
    scan_weights, rest_weights = weights
    (norm_scale, taps, tap_bias, step_bias, decay_log, skip_gain, gate_gain) = params
    count = lax.axis_size("context")
    length, width = entry[0].shape
    inner, mixed, heads = gate_gain.shape[1], taps.shape[1], decay_log.shape[1]
    size = (mixed - inner) // 2
    inner_total = inner * lax.axis_size("tensor")
    combine = len(entry) > 1
    results = [
        ((length, 1), wide), ((length, width), low), ((length, mixed), wide), ((length, heads), wide),
    ]
    norm_one, normed, conv_pre, step_pre, *rest = call(
        functools.partial(enter_body, bit_order(), inner_total, mixed, combine),
        (*entry, norm_scale, *scan_weights),
        results + [((length, width), wide)] * combine,
        flops=2 * length * width * mixed,
    )
    hidden_in = rest[0] if combine else entry[0]
    edge = shifted(conv_pre[length - 8 :], "context", 1)
    lin, dt, cs, cst, local_state, low_state, block_decay = call(
        functools.partial(states_body, inner),
        (conv_pre, edge, taps, tap_bias, step_pre, step_bias, decay_log),
        [
            ((length, mixed), wide), ((length, heads), wide), ((length, heads), wide),
            ((heads, length), wide), ((size, inner), wide), ((size, inner), low), ((1, inner), wide),
        ],
        [((length + 8, mixed), wide)],
        flops=4 * 10**9,
    )
    y_near = call(
        functools.partial(intra_body, inner),
        (lin, dt, cs, cst, skip_gain),
        [((length, inner), wide)],
        flops=6 * 10**9,
    )[0]
    begun = begin(y_near)
    carried, _ = chained(block_decay, local_state, low_state, 1, (y_near,))
    gate_pre, y, squares, mine = call(
        functools.partial(leave_body, inner, count),
        (lin, cs, y_near, carried, normed, gate_gain, *rest_weights),
        [
            ((length, inner), wide), ((length, inner), wide), ((length, 1), wide),
            ((length, width), low),
        ],
        flops=5 * 10**9,
        after=begun[:1],
    )
    squares_other = swapped(squares, "tensor", 1)
    other = swapped(mine, "tensor", 1)
    stored = (
        hidden_in, norm_one, normed, conv_pre, edge, step_pre, lin, dt, cs, cst, block_decay, carried,
        gate_pre, y, squares, squares_other, mine, other, y_near,
    )
    return (hidden_in, mine, other, squares, squares_other), stored, begun


def layer_backward(gradient, weights, params, stored, last, after):
    scan_weights, rest_weights = weights
    (norm_scale, taps, tap_bias, step_bias, decay_log, skip_gain, gate_gain) = params
    (
        hidden_in, norm_one, normed, conv_pre, edge, step_pre, lin, dt, cs, cst, block_decay, carried,
        gate_pre, y, squares, squares_other, mine, other, _,
    ) = stored
    count = lax.axis_size("context")
    length, width = gradient.shape
    inner, mixed, heads = gate_gain.shape[1], taps.shape[1], decay_log.shape[1]
    size = (mixed - inner) // 2
    inner_total = inner * lax.axis_size("tensor")
    grad_low, normed_out, gate_grad, gy, gz, grad_state, low_state = call(
        functools.partial(gate_back_body, inner, inner_total, count),
        (gradient, lin, cs, y, gate_pre, gate_gain, squares, squares_other, mine, other, *rest_weights),
        [
            ((length, width), low), ((length, inner), low), ((1, inner), wide),
            ((length, inner), wide), ((length, inner), low), ((size, inner), wide), ((size, inner), low),
        ],
        flops=4 * 10**9,
        after=after[:1],
    )
    following, chain_end = chained(block_decay, grad_state, low_state, -1)
    rest_total, rest_mine, rest_end = reduced_late(*product_grads((grad_low, normed_out), (normed, gz)))
    gxw, gb, gc, gcs = call(
        functools.partial(intra_back_body, inner),
        (gy, lin, dt, cs, cst, carried),
        [((length, inner), wide), ((length, size), wide), ((length, size), wide), ((length, heads), wide)],
        [((8, 128), wide), ((max(128, heads), length), wide)],
        flops=12 * 10**9,
    )
    glin, gstep, taps_grad, tap_bias_grad, heads_grad = call(
        functools.partial(scan_back_body, inner),
        (
            following, carried, gy, gxw, gb, gc, gcs, lin, conv_pre, edge, dt, cs, step_pre, step_bias,
            decay_log, skip_gain, taps,
        ),
        [
            ((length, mixed), wide), ((length, heads), low), (taps.shape, wide), ((1, mixed), wide),
            ((8, heads), wide),
        ],
        [((length + 8, mixed), wide)],
        flops=6 * 10**9,
        after=(rest_total,),
    )
    halo = shifted(glin[:8], "context", -1)
    width_operands = (gz, *scan_weights, *rest_weights)
    wide_shape = (length, scan_weights[0].shape[-1])
    enter_operands = (glin, halo, taps, gstep)
    enter_scratch = [((length + 8, mixed), wide)]
    if last:
        gscan = call(
            functools.partial(enter_back_body, None), enter_operands, [(wide_shape, low)], enter_scratch
        )[0]
        scan_cut = product_grads((normed, gscan))
        mine_back = call(
            functools.partial(width_body, bit_order()),
            (gscan, *width_operands),
            [((length, width), low)],
            flops=4 * 10**9,
            after=(after[1], *scan_cut),
        )[0]
        scan_total, scan_mine, (_, scan_end) = reduced(
            *scan_cut, first_after=(mine_back,), after=(rest_mine,)
        )
    else:
        gscan, mine_back = call(
            functools.partial(enter_back_body, bit_order()),
            enter_operands + width_operands,
            [(wide_shape, low), ((length, width), low)],
            enter_scratch,
            flops=4 * 10**9,
        )
    other_back = swapped(mine_back, "tensor", 1)
    if not last:
        scan_cut = product_grads((normed, gscan), after=(mine_back,))
        scan_total, scan_mine, scan_end = reduced_late(*scan_cut)
    grad_hidden, prenorm_grad = call(
        norm_back_body,
        (gradient, mine_back, other_back, hidden_in, norm_one, norm_scale),
        [((length, width), wide), ((1, width), wide)],
        after=(scan_total,) if last else (),
    )
    def whole_states(part, first):
        here = part[..., first : first + mixed - inner]
        here = (here.astype(wide) + swapped(here, "tensor", 1).astype(wide)).astype(low)
        return jnp.concatenate(
            [part[..., :first], here, part[..., first + mixed - inner :]], axis=-1
        )

    if last:
        rest_part, scan_part = rest_end(rest_mine), scan_end(whole_states(scan_mine, inner))
        rest_part = jnp.concatenate([rest_part, swapped(rest_part, "context", 1)])
        large_part = (rest_part, scan_part)
    else:
        def large_part(after, later):
            shape = (rest_mine.shape[0], rest_mine.shape[1] + scan_mine.shape[1])
            part = call(joined_body, (rest_mine, scan_mine), [(shape, low)], after=after)[0]
            part = whole_states(rest_end(part, later), rest_mine.shape[1] + inner)
            return (jnp.concatenate([part, swapped(part, "context", 1)]),)
    small_part = (
        prenorm_grad[0],
        taps_grad[:, :inner],
        tap_bias_grad[0, :inner],
        taps_grad[:, inner:],
        tap_bias_grad[0, inner:],
        heads_grad[0],
        heads_grad[1],
        heads_grad[2],
        gate_grad[0],
    )
    return (grad_hidden, large_part, small_part, (rest_mine, scan_mine, scan_total, rest_total))


def on_device(
    hidden,
    cotangent,
    norm_gain,
    inner_proj,
    state_proj,
    step_proj,
    inner_conv,
    inner_bias,
    state_conv,
    state_bias,
    step_bias,
    decay_log,
    skip_gain,
    gate_gain,
    out_proj,
):
    layers_here = inner_proj.shape[0]
    me, count = lax.axis_index("context"), lax.axis_size("context")
    rows = inner_proj.shape[1] // count

    def quarter(value, axis):
        return lax.dynamic_slice_in_dim(value, me * rows, rows, axis)

    inner, heads = gate_gain.shape[1], decay_log.shape[1]
    mixed = inner + state_proj.shape[2]
    inner_q, state_q, step_q = (quarter(v, 1) for v in (inner_proj, state_proj, step_proj))
    step_q = jnp.pad(step_q, ((0, 0), (0, 0), (0, -(mixed + heads) % 128)))
    out_q = quarter(out_proj, 2)

    def own_rows(layer):
        scan = jnp.concatenate([inner_q[layer, :, 1], state_q[layer], step_q[layer]], axis=1)
        return scan, jnp.concatenate([inner_q[layer, :, 0], out_q[layer].T], axis=1)

    def token(value):
        return value[(slice(0, 1),) * value.ndim].reshape(1, 1).astype(low) * 0

    scan_own, rest_own = own_rows(0)
    scan_all = gathered(scan_own)
    layer_weights = [(spread(scan_all), spread(gathered(rest_own)))]

    def begin(layer, near):
        if layer == layers_here:
            return ()
        own = jnp.concatenate(own_rows(layer), axis=1) + token(scan_all)
        whole = lax.all_gather(own, "dp", axis=0, tiled=True)
        width = scan_all.shape[1]
        return whole[:, :width] + token(near), whole[:, width:]

    taps = jnp.concatenate([inner_conv, state_conv], axis=-1)
    tap_bias = jnp.concatenate([inner_bias, state_bias], axis=-1)
    gains = to_local(norm_gain)
    entry = (to_local(hidden[0]).astype(wide),)
    kept_stored = []
    layer_params = []
    for layer in range(layers_here):
        layer_params.append(
            tuple(
                v[layer] if v.ndim == 3 else v[layer][None]
                for v in (gains, taps, tap_bias, step_bias, decay_log, skip_gain, gate_gain)
            )
        )
        entry, stored, begun = layer_forward(
            entry, layer_weights[layer], layer_params[layer], functools.partial(begin, layer + 1)
        )
        kept_stored.append(stored)
        if layer + 1 < layers_here:
            scan, rest = begun
            layer_weights.append((spread(scan), spread(rest + token(entry[1]))))
    gradient = to_local(cotangent[0]).astype(wide)
    large_grads = [None] * layers_here
    after = ()
    small_grads = [None] * layers_here
    for layer in reversed(range(layers_here)):
        gradient, large_grads[layer], small_grads[layer], after = layer_backward(
            gradient, layer_weights[layer], layer_params[layer], kept_stored[layer], layer == 0, after
        )
    stacked = [jnp.stack([member[i] for member in small_grads]) for i in range(9)]
    stacked[0] = from_local(stacked[0])
    later = token(after[2]).astype(wide)[0, 0]
    stacked = [part + later for part in stacked]
    current, mine, other, squares, squares_other = entry
    norm_two = gate_norm(
        gate_gain.shape[1] * lax.axis_size("tensor"), squares + later, squares_other
    )
    current = current + norm_two * (mine.astype(wide) + other.astype(wide))
    output = from_local(current.astype(low))
    stacked[3:5] = everywhere(stacked[3:5], ("tensor",))
    summed = everywhere(stacked, ("dp", "context"))
    large_grads = [part(after[2:3], later) if callable(part) else part for part in large_grads]
    inner_grad, state_grad, step_grad, outer_grad = finish(large_grads, inner, mixed, heads)
    return (
        output[None],
        from_local(gradient.astype(low))[None],
        summed[0],
        inner_grad,
        state_grad,
        step_grad,
        summed[1],
        summed[2],
        summed[3],
        summed[4],
        summed[5],
        summed[6],
        summed[7],
        summed[8],
        outer_grad,
    )


def solution(mesh):
    return jax.shard_map(
        on_device,
        mesh=mesh,
        in_specs=(
            P("dp", "context", None),
            P("dp", "context", None),
            P(),
            P(None, "dp", None, "tensor"),
            P(None, "dp", None),
            P(None, "dp", "tensor"),
            P(None, None, "tensor"),
            P(None, "tensor"),
            P(),
            P(),
            P(None, "tensor"),
            P(None, "tensor"),
            P(None, "tensor"),
            P(None, "tensor"),
            P(None, "tensor", "dp"),
        ),
        out_specs=(
            P("dp", "context", None),
            P("dp", "context", None),
            P(),
            P(None, "dp", None, "tensor"),
            P(None, "dp", None),
            P(None, "dp", "tensor"),
            P(None, None, "tensor"),
            P(None, "tensor"),
            P(),
            P(),
            P(None, "tensor"),
            P(None, "tensor"),
            P(None, "tensor"),
            P(None, "tensor"),
            P(None, "tensor", "dp"),
        ),
        check_vma=False,
    )
```
